256 devices in a mesh: energy: 64 (over x, z_hi, y), space: 4 (over z_lo, core).
Axes of the slice: x: 4, y: 4, z: 8 (z_hi: 4, z_lo: 2; z = z_hi * 2 + z_lo), core: 2. Of those that a mesh axis runs over, the one named last changes fastest.
Arguments:
- screening: bfloat16 [64, 8, 3, 2, 128, 128], P('energy', 'space'), may hold values from -0.21875 to 0.21875
- polarization: bfloat16 [64, 8, 3, 2, 128, 128], P('energy', 'space'), may hold values from -6 to 6
- propagator: bfloat16 [64, 8, 3, 2, 128, 128], P('energy', 'space'), may hold values from -0.21875 to 0.21875
Outputs:
- dressed: bfloat16 [64, 8, 3, 2, 128, 128], P('energy', 'space')
The draws below stay inside these ranges and needn't reach their ends.
All inputs are finite; a program needn't handle non-finite values.
Results may differ from the reference program's by a relative error of at most 0.015.
Values may be sent and summed in bfloat16 or wider, within the bound.
A program may use at most 64 MiB of HBM per device.

```python
import jax
import jax.numpy as jnp
from jax import lax

B = 128
NE = 64
NB = 8


def levels(stream_key, dims, shards, low, largest):
    level = 1.0
    for position, parts in shards:
        steps = jax.random.uniform(jax.random.fold_in(jax.random.fold_in(stream_key, 6), position), (parts,), jnp.float32, low / len(shards), largest / len(shards))
        level = level * jnp.repeat(jnp.exp(steps), dims[position] // parts).reshape((-1,) + (1,) * (len(dims) - 1 - position))
    return level


def bell_draw(key, extent, scale, limit, pieces=(), held_as=jnp.bfloat16):
    factor_of = levels(key, extent, pieces, -0.22, 0.18) if pieces else 1.0
    entries = jax.random.normal(key, extent, jnp.float32) * scale * factor_of
    return jnp.minimum(jnp.maximum(entries, -limit), limit).astype(held_as)


def setup_inputs(seed: int = 0) -> dict:
    arg_keys = jax.random.split(jax.random.key(seed), 4)
    screening = bell_draw(arg_keys[0], (NE, NB, 3, 2, B, B), (6 * B) ** -0.5, 0.21875, ((0, 64), (1, 4)))
    polarization = bell_draw(arg_keys[1], (NE, NB, 3, 2, B, B), 1.0, 6.0, ((0, 64), (1, 4)))
    propagator = bell_draw(arg_keys[2], (NE, NB, 3, 2, B, B), (6 * B) ** -0.5, 0.21875, ((0, 64), (1, 4)))
    return {"screening": screening, "polarization": polarization, "propagator": propagator}


def clip_edges(banded, first_row, row_total):
    row_count = banded.shape[1]
    row_index = first_row + jnp.arange(row_count, dtype=jnp.int32)
    band_index = jnp.arange(3, dtype=jnp.int32)
    dropped = ((band_index[None, :] == 0) & (row_index[:, None] == 0)) | ((band_index[None, :] == 2) & (row_index[:, None] == row_total - 1))
    keep_mask = jnp.where(dropped, 0.0, 1.0).astype(banded.dtype)
    return banded * keep_mask[None, :, :, None, None, None]


def complex_product(first, second, adjoint):
    first_real = first[..., 0, :, :].astype(jnp.float32)
    first_imag = first[..., 1, :, :].astype(jnp.float32)
    second_real = second[..., 0, :, :].astype(jnp.float32)
    second_imag = second[..., 1, :, :].astype(jnp.float32)
    if adjoint:
        form = "...ij,...kj->...ik"
        real_part = jnp.einsum(form, first_real, second_real) + jnp.einsum(form, first_imag, second_imag)
        imag_part = jnp.einsum(form, first_imag, second_real) - jnp.einsum(form, first_real, second_imag)
    else:
        form = "...ij,...jk->...ik"
        real_part = jnp.einsum(form, first_real, second_real) - jnp.einsum(form, first_imag, second_imag)
        imag_part = jnp.einsum(form, first_real, second_imag) + jnp.einsum(form, first_imag, second_real)
    return jnp.stack([real_part, imag_part], axis=-3)


def pick_rows(banded, start, row_count, band):
    sliced = lax.slice_in_dim(banded, start, start + row_count, axis=banded.ndim - 5)
    return sliced[..., band, :, :, :]


def sandwich(outside, between):
    row_count = outside.shape[-5] - 2
    products = {}
    for offset in range(-2, 3):
        summed = None
        for inner in range(-1, 2):
            if abs(offset - inner) <= 1:
                term = complex_product(pick_rows(outside, 1, row_count, inner + 1), pick_rows(between, 1 + inner, row_count, offset - inner + 1), False)
                summed = term if summed is None else summed + term
        products[offset] = summed.astype(jnp.bfloat16)
    bands = []
    for target in range(-1, 2):
        summed = None
        for offset in range(target - 1, target + 2):
            term = complex_product(products[offset], pick_rows(outside, 1 + target, row_count, offset - target + 1), True)
            summed = term if summed is None else summed + term
        bands.append(summed)
    return jnp.stack(bands, axis=-4)


def pad_rows(banded):
    return jnp.pad(banded, ((0, 0), (1, 1), (0, 0), (0, 0), (0, 0), (0, 0)))


def reference(screening, polarization, propagator):
    energy_count = screening.shape[0]
    row_total = screening.shape[1]
    order = screening.shape[-1]
    screen_masked = clip_edges(screening, 0, row_total)
    polar_masked = clip_edges(polarization, 0, row_total)
    propa_masked = clip_edges(propagator, 0, row_total)
    screened = lax.map(lambda pair: sandwich(pair[0], pair[1]).astype(jnp.bfloat16), (pad_rows(screen_masked), pad_rows(polar_masked)))
    factor = (3.0 * order / energy_count) ** 0.5

    def convolve_row(pair):
        propa_row, screen_row = pair
        propa_complex = propa_row[:, :, 0].astype(jnp.float32) + 1j * propa_row[:, :, 1].astype(jnp.float32)
        screen_complex = screen_row[:, :, 0].astype(jnp.float32) + 1j * screen_row[:, :, 1].astype(jnp.float32)
        spectrum = jnp.fft.fft(propa_complex, n=2 * energy_count, axis=0) * jnp.fft.fft(screen_complex, n=2 * energy_count, axis=0)
        summed = jnp.fft.ifft(spectrum, axis=0)[:energy_count] * factor
        return jnp.stack([jnp.real(summed), jnp.imag(summed)], axis=2).astype(jnp.bfloat16)

    sigma_rows = lax.map(convolve_row, (jnp.moveaxis(propa_masked, 1, 0), jnp.moveaxis(screened, 1, 0)))
    sigma = jnp.moveaxis(sigma_rows, 0, 1)
    dressed = lax.map(lambda pair: sandwich(pair[0], pair[1]).astype(jnp.bfloat16), (pad_rows(propa_masked), pad_rows(sigma)))
    return dressed
```

```python
import math

import jax
import jax.numpy as jnp
import ml_dtypes
import numpy as np
from jax import lax
from jax.experimental import pallas as pl
from jax.experimental.pallas import tpu as pltpu
from jax.sharding import PartitionSpec as P

MESH = pl.DeviceIdType.MESH
B = 128
NE = 64
NS = 4
HALF = NE // 2
F32 = jnp.float32
BF16 = jnp.bfloat16


def split_np(table):
    upper = table.astype(ml_dtypes.bfloat16)
    lower = (table - upper.astype(np.float64)).astype(ml_dtypes.bfloat16)
    return upper, lower


def tables(factor):
    freq = np.arange(2 * NE)
    time = np.arange(NE)
    angle = (freq[:, None] * time[None, :] % (2 * NE)) * (math.pi / NE)
    cos, sin = np.cos(angle), np.sin(angle)
    fwd = np.block([[cos, sin], [-sin, cos]])
    back = np.block([[cos.T, -sin.T], [sin.T, cos.T]]) * (factor / (2 * NE))
    fh, fl = split_np(fwd)
    bh, bl = split_np(back)
    return np.concatenate([fh, fl], 1), np.concatenate([bh, bh, bl], 1)


def dot(a, b):
    return jnp.dot(a, b, preferred_element_type=F32)


def dot_nt(a, b):
    return lax.dot_general(a, b, (((1,), (1,)), ((), ())), preferred_element_type=F32)


def wide(ref, row, band):
    return jnp.concatenate([ref[row, band, 0], ref[row, band, 1]], axis=1)


def embed(ref, row, band):
    re, im = ref[row, band, 0], ref[row, band, 1]
    return jnp.concatenate(
        [jnp.concatenate([re, im], axis=1), jnp.concatenate([-im, re], axis=1)], axis=0
    )


def sandwich_row(outer, inner, row):
    products = {}
    for offset in range(-2, 3):
        steps = [k for k in (-1, 0, 1) if abs(offset - k) <= 1]
        lhs = jnp.concatenate([wide(outer, row, k + 1) for k in steps], axis=1)
        rhs = jnp.concatenate([embed(inner, row + k, offset - k + 1) for k in steps], axis=0)
        products[offset] = dot(lhs, rhs).astype(BF16)
    bands = []
    for target in (-1, 0, 1):
        offsets = range(target - 1, target + 2)
        lhs = jnp.concatenate([products[d] for d in offsets], axis=1)
        rhs = jnp.concatenate([embed(outer, row + target, d - target + 1) for d in offsets], axis=1)
        bands.append(dot_nt(lhs, rhs))
    return bands


def pack(re, im):
    re, im = re.reshape(16, 8, B), im.reshape(16, 8, B)
    low = lax.broadcasted_iota(jnp.int32, (16, 8, B), 1) < 4
    even = jnp.where(low, re, pltpu.roll(im, 4, 1))
    odd = jnp.where(low, pltpu.roll(re, 4, 1), im)
    return jnp.stack([even, odd], axis=1).reshape(HALF, 8, B)


def unpack(packed):
    pairs = packed.reshape(16, 2, 8, B)
    even, odd = pairs[:, 0], pairs[:, 1]
    low = lax.broadcasted_iota(jnp.int32, (16, 8, B), 1) < 4
    re = jnp.where(low, even, pltpu.roll(odd, 4, 1))
    im = jnp.where(low, pltpu.roll(even, 4, 1), odd)
    return re.reshape(B, B), im.reshape(B, B)


def kernel(
    w_hbm, p_hbm, g_hbm, fwd_ref, back_ref, out_ref,
    w4, p4, g4, s4, g_send, g_recv, s_send, s_recv, c_send, c_recv, c_prev, c_next,
    g_spec, stage, load_sem, edge_send, edge_recv, swap_send, swap_recv,
):
    e = lax.axis_index("energy")
    s = lax.axis_index("space")
    barrier = pltpu.get_barrier_semaphore()
    loads = [
        pltpu.make_async_copy(src, dst.at[pl.ds(1, 2)], load_sem.at[i])
        for i, (src, dst) in enumerate(((g_hbm, g4), (w_hbm, w4), (p_hbm, p4)))
    ]
    for load in loads:
        load.start()

    def greet(i, carry):
        pl.semaphore_signal(barrier, inc=1, device_id=(lax.rem(e + i, NE), s), device_id_type=MESH)
        return carry

    @pl.when(s > 0)
    def _():
        pl.semaphore_signal(barrier, inc=1, device_id=(e, s - 1), device_id_type=MESH)

    @pl.when(s < NS - 1)
    def _():
        pl.semaphore_signal(barrier, inc=1, device_id=(e, s + 1), device_id_type=MESH)

    lax.fori_loop(1, NE, greet, 0)

    for load in loads:
        load.wait()

    @pl.when(s == 0)
    def _():
        for ref in (w4, p4, g4):
            ref[0] = jnp.zeros(ref.shape[1:], BF16)
            ref[1, 0] = jnp.zeros(ref.shape[2:], BF16)
        c_prev[...] = jnp.zeros(c_prev.shape, BF16)

    @pl.when(s == NS - 1)
    def _():
        for ref in (w4, p4, g4):
            ref[3] = jnp.zeros(ref.shape[1:], BF16)
            ref[2, 2] = jnp.zeros(ref.shape[2:], BF16)
        c_next[...] = jnp.zeros(c_next.shape, BF16)

    for c in range(3):
        for half in range(2):
            band = c if half == 0 else 2 - c
            re = g4[1 + half, band, 0].astype(F32)
            im = g4[1 + half, band, 1].astype(F32)
            g_send[c, pl.ds(half * HALF, HALF)] = pack(re, im).astype(BF16)

    pl.semaphore_wait(barrier, NE - 1 + (s > 0).astype(jnp.int32) + (s < NS - 1).astype(jnp.int32))

    def to_next(src, dst, i):
        return pltpu.make_async_remote_copy(
            src, dst, edge_send.at[i], edge_recv.at[i], device_id=(e, s + 1), device_id_type=MESH
        )

    def to_prev(src, dst, i):
        return pltpu.make_async_remote_copy(
            src, dst, edge_send.at[i], edge_recv.at[i], device_id=(e, s - 1), device_id_type=MESH
        )

    w_next, w_prev = to_next(w4.at[2], w4.at[0], 0), to_prev(w4.at[1], w4.at[3], 1)
    p_next, p_prev = to_next(p4.at[2], p4.at[0], 2), to_prev(p4.at[1], p4.at[3], 3)
    g_next, g_prev = to_next(g4.at[2], g4.at[0], 4), to_prev(g4.at[1], g4.at[3], 5)
    c_nexts = [to_next(c_recv.at[c, pl.ds(HALF, HALF)], c_prev.at[c], 6 + c) for c in range(3)]
    c_prevs = [to_prev(c_recv.at[c, pl.ds(0, HALF)], c_next.at[c], 9 + c) for c in range(3)]

    def edges(nexts, prevs, action):
        forward, backward = (prevs, nexts) if action == "wait_recv" else (nexts, prevs)

        @pl.when(s < NS - 1)
        def _():
            for copy in forward:
                getattr(copy, action)()

        @pl.when(s > 0)
        def _():
            for copy in backward:
                getattr(copy, action)()

    def swap(send, recv, slot):
        def body(i, carry):
            to = lax.rem(e + i, NE)
            pltpu.make_async_remote_copy(
                send.at[:, to], recv.at[:, e], swap_send.at[slot], swap_recv.at[slot],
                device_id=(to, s), device_id_type=MESH,
            ).start()
            return carry

        lax.fori_loop(1, NE, body, 0)
        pltpu.make_async_copy(send.at[:, e], recv.at[:, e], swap_recv.at[slot]).start()

    def wait_swap(recv, slot):
        pltpu.make_async_copy(recv, recv, swap_recv.at[slot]).wait()

    def wait_sent(send, slot):
        part = send.at[:, pl.ds(0, NE - 1)]
        pltpu.make_async_copy(part, part, swap_send.at[slot]).wait()

    edges([w_next, p_next], [w_prev, p_prev], "start")
    swap(g_send, g_recv, 0)
    edges([w_next, p_next], [w_prev, p_prev], "wait_recv")

    for half in range(2):
        bands = sandwich_row(w4, p4, 1 + half)
        for band in range(3):
            c = band if half == 0 else 2 - band
            s_send[c, pl.ds(half * HALF, HALF)] = pack(
                bands[band][:, :B], bands[band][:, B:]
            ).astype(BF16)
    swap(s_send, s_recv, 1)
    edges([g_next], [g_prev], "start")

    def spectrum(recv, c):
        stage[...] = recv[c].astype(F32).reshape(NE * 8, B)
        rows = [stage[pl.ds(r, NE, stride=8), :].astype(BF16) for r in range(8)]
        data = jnp.concatenate(
            [jnp.concatenate(rows[:4], axis=1), jnp.concatenate(rows[4:], axis=1)], axis=0
        )
        return dot(fwd_ref[...], jnp.concatenate([data, data], axis=0))

    wait_swap(g_recv, 0)
    for c in range(3):
        g_spec[c] = spectrum(g_recv, c)
    wait_swap(s_recv, 1)
    for c in range(3):
        spec = spectrum(s_recv, c)
        sr, si = spec[: 2 * NE], spec[2 * NE :]
        gr, gi = g_spec[c, : 2 * NE], g_spec[c, 2 * NE :]
        both = jnp.concatenate([gr * sr - gi * si, gr * si + gi * sr], axis=0)
        upper = both.astype(BF16)
        lower = (both - upper.astype(F32)).astype(BF16)
        sums = dot(back_ref[...], jnp.concatenate([upper, lower, upper], axis=0))
        for r in range(4):
            stage[pl.ds(r, NE, stride=8), :] = sums[:NE, r * B : (r + 1) * B]
            stage[pl.ds(r + 4, NE, stride=8), :] = sums[NE:, r * B : (r + 1) * B]
        c_send[c] = stage[...].reshape(NE, 8, B).astype(BF16)
    swap(c_send, c_recv, 2)
    edges([g_next], [g_prev], "wait_recv")
    wait_swap(c_recv, 2)
    edges(c_nexts, c_prevs, "start")

    def place(packed, row, band):
        re, im = unpack(packed.astype(F32))
        s4[row, band, 0] = re.astype(BF16)
        s4[row, band, 1] = im.astype(BF16)

    for c in range(3):
        place(c_recv[c, pl.ds(0, HALF)], 1, c)
        place(c_recv[c, pl.ds(HALF, HALF)], 2, 2 - c)
    edges(c_nexts, c_prevs, "wait_recv")
    for c in range(3):
        place(c_prev[c], 0, 2 - c)
        place(c_next[c], 3, c)
    for half in range(2):
        bands = sandwich_row(g4, s4, 1 + half)
        for band in range(3):
            out_ref[half, band, 0] = bands[band][:, :B].astype(BF16)
            out_ref[half, band, 1] = bands[band][:, B:].astype(BF16)

    edges([w_next, p_next, g_next, *c_nexts], [w_prev, p_prev, g_prev, *c_prevs], "wait_send")
    wait_sent(g_send, 0)
    wait_sent(s_send, 1)
    wait_sent(c_send, 2)


def local(screening, polarization, propagator):
    fwd, back = tables((3.0 * B / NE) ** 0.5)
    four = pltpu.VMEM((4, 3, 2, B, B), BF16)
    full = pltpu.VMEM((3, NE, 8, B), BF16)
    rim = pltpu.VMEM((3, HALF, 8, B), BF16)
    hbm = pl.BlockSpec(memory_space=pl.ANY)
    vmem = pl.BlockSpec(memory_space=pltpu.VMEM)
    out = pl.pallas_call(
        kernel,
        name="self_energy",
        out_shape=jax.ShapeDtypeStruct((2, 3, 2, B, B), BF16),
        in_specs=[hbm, hbm, hbm, vmem, vmem],
        out_specs=vmem,
        scratch_shapes=[
            four, four, four, four,
            full, full, full, full, full, full, rim, rim,
            pltpu.VMEM((3, 4 * NE, 4 * B), F32),
            pltpu.VMEM((NE * 8, B), F32),
            pltpu.SemaphoreType.DMA((3,)),
            pltpu.SemaphoreType.DMA((12,)),
            pltpu.SemaphoreType.DMA((12,)),
            pltpu.SemaphoreType.DMA((3,)),
            pltpu.SemaphoreType.DMA((3,)),
        ],
        compiler_params=pltpu.CompilerParams(
            collective_id=0, has_side_effects=True, vmem_limit_bytes=48 << 20
        ),
    )(screening[0], polarization[0], propagator[0], jnp.asarray(fwd), jnp.asarray(back))
    return out[None]


def solution(mesh):
    spec = P("energy", "space", None, None, None, None)
    return jax.shard_map(
        local, mesh=mesh, in_specs=(spec, spec, spec), out_specs=spec, check_vma=False
    )
```

```python
import math

import jax
import jax.numpy as jnp
import ml_dtypes
import numpy as np
from jax import lax
from jax.experimental import pallas as pl
from jax.experimental.pallas import tpu as pltpu
from jax.sharding import PartitionSpec as P

MESH = pl.DeviceIdType.MESH
B = 128
NE = 64
NS = 4
HALF = NE // 2
F32 = jnp.float32
BF16 = jnp.bfloat16


def split_np(table):
    upper = table.astype(ml_dtypes.bfloat16)
    lower = (table - upper.astype(np.float64)).astype(ml_dtypes.bfloat16)
    return upper, lower


def tables(factor):
    freq = np.arange(2 * NE)
    time = np.arange(NE)
    angle = (freq[:, None] * time[None, :] % (2 * NE)) * (math.pi / NE)
    cos, sin = np.cos(angle), np.sin(angle)
    fwd = np.block([[cos, sin], [-sin, cos]])
    back = np.block([[cos.T, -sin.T], [sin.T, cos.T]]) * (factor / (2 * NE))
    fh, fl = split_np(fwd)
    bh, bl = split_np(back)
    return np.concatenate([fh, fl], 1), np.concatenate([bh, bh, bl], 1)


def dot(a, b):
    return jnp.dot(a, b, preferred_element_type=F32)


def dot_nt(a, b):
    return lax.dot_general(a, b, (((1,), (1,)), ((), ())), preferred_element_type=F32)


def wide(ref, row, band):
    return jnp.concatenate([ref[row, band, 0], ref[row, band, 1]], axis=1)


def embed(ref, row, band):
    re, im = ref[row, band, 0], ref[row, band, 1]
    return jnp.concatenate(
        [jnp.concatenate([re, im], axis=1), jnp.concatenate([-im, re], axis=1)], axis=0
    )


def products_row(outer, inner, row):
    products = {}
    for offset in range(-2, 3):
        steps = [k for k in (-1, 0, 1) if abs(offset - k) <= 1]
        lhs = jnp.concatenate([wide(outer, row, k + 1) for k in steps], axis=1)
        rhs = jnp.concatenate([embed(inner, row + k, offset - k + 1) for k in steps], axis=0)
        products[offset] = dot(lhs, rhs).astype(BF16)
    return products


def close_row(products, outer, row, band):
    offsets = range(band - 2, band + 1)
    lhs = jnp.concatenate([products[d] for d in offsets], axis=1)
    rhs = jnp.concatenate([embed(outer, row + band - 1, d - band + 2) for d in offsets], axis=1)
    return dot_nt(lhs, rhs)


def pack(re, im):
    re, im = re.reshape(16, 8, B), im.reshape(16, 8, B)
    low = lax.broadcasted_iota(jnp.int32, (16, 8, B), 1) < 4
    even = jnp.where(low, re, pltpu.roll(im, 4, 1))
    odd = jnp.where(low, pltpu.roll(re, 4, 1), im)
    return jnp.stack([even, odd], axis=1).reshape(HALF, 8, B)


def unpack(packed):
    pairs = packed.reshape(16, 2, 8, B)
    even, odd = pairs[:, 0], pairs[:, 1]
    low = lax.broadcasted_iota(jnp.int32, (16, 8, B), 1) < 4
    re = jnp.where(low, even, pltpu.roll(odd, 4, 1))
    im = jnp.where(low, pltpu.roll(even, 4, 1), odd)
    return re.reshape(B, B), im.reshape(B, B)


def kernel(
    w_hbm, p_hbm, g_hbm, fwd_hbm, back_hbm, out_ref,
    w4, p4, g4, s4, g_send, g_recv, s_send, s_recv, c_send, c_recv, c_prev, c_next,
    fwd_ref, back_ref, g_spec, stage, load_sem, edge_send, edge_recv, swap_send, swap_recv,
):
    e = lax.axis_index("energy")
    s = lax.axis_index("space")
    barrier = pltpu.get_barrier_semaphore()
    loads = [
        pltpu.make_async_copy(src, dst.at[pl.ds(1, 2)], load_sem.at[i])
        for i, (src, dst) in enumerate(((g_hbm, g4), (w_hbm, w4), (p_hbm, p4)))
    ]
    table_loads = [
        pltpu.make_async_copy(fwd_hbm, fwd_ref, load_sem.at[3]),
        pltpu.make_async_copy(back_hbm, back_ref, load_sem.at[4]),
    ]
    for load in loads + table_loads:
        load.start()

    def greet(i, carry):
        pl.semaphore_signal(barrier, inc=1, device_id=(lax.rem(e + i, NE), s), device_id_type=MESH)
        return carry

    @pl.when(s > 0)
    def _():
        pl.semaphore_signal(barrier, inc=1, device_id=(e, s - 1), device_id_type=MESH)

    @pl.when(s < NS - 1)
    def _():
        pl.semaphore_signal(barrier, inc=1, device_id=(e, s + 1), device_id_type=MESH)

    lax.fori_loop(1, NE, greet, 0)

    first, last = s == 0, s == NS - 1
    low = e < HALF
    idle = (first & low) | (last & jnp.logical_not(low))
    for load in loads:
        load.wait()

    @pl.when(first)
    def _():
        for ref in (w4, p4, g4):
            ref[0] = jnp.zeros(ref.shape[1:], BF16)
            ref[1, 0] = jnp.zeros(ref.shape[2:], BF16)
        c_prev[...] = jnp.zeros(c_prev.shape, BF16)
        c_recv[0, :HALF] = jnp.zeros((HALF, 8, B), BF16)

    @pl.when(last)
    def _():
        for ref in (w4, p4, g4):
            ref[3] = jnp.zeros(ref.shape[1:], BF16)
            ref[2, 2] = jnp.zeros(ref.shape[2:], BF16)
        c_next[...] = jnp.zeros(c_next.shape, BF16)
        c_recv[0, HALF:] = jnp.zeros((HALF, 8, B), BF16)

    pl.semaphore_wait(barrier, NE - 1 + (s > 0).astype(jnp.int32) + (s < NS - 1).astype(jnp.int32))

    def to_next(src, dst, i):
        return pltpu.make_async_remote_copy(
            src, dst, edge_send.at[i], edge_recv.at[i], device_id=(e, s + 1), device_id_type=MESH
        )

    def to_prev(src, dst, i):
        return pltpu.make_async_remote_copy(
            src, dst, edge_send.at[i], edge_recv.at[i], device_id=(e, s - 1), device_id_type=MESH
        )

    groups = (pl.ds(1, 2), pl.ds(0, 1))
    w_next, w_prev = to_next(w4.at[2], w4.at[0], 0), to_prev(w4.at[1], w4.at[3], 1)
    p_next, p_prev = to_next(p4.at[2], p4.at[0], 2), to_prev(p4.at[1], p4.at[3], 3)
    g_next, g_prev = to_next(g4.at[2], g4.at[0], 4), to_prev(g4.at[1], g4.at[3], 5)
    c_nexts = [
        to_next(c_recv.at[part, pl.ds(HALF, HALF)], c_prev.at[part], 6 + k)
        for k, part in enumerate(groups)
    ]
    c_prevs = [
        to_prev(c_recv.at[part, pl.ds(0, HALF)], c_next.at[part], 8 + k)
        for k, part in enumerate(groups)
    ]

    def edges(nexts, prevs, action):
        forward, backward = (prevs, nexts) if action == "wait_recv" else (nexts, prevs)

        @pl.when(s < NS - 1)
        def _():
            for copy in forward:
                getattr(copy, action)()

        @pl.when(s > 0)
        def _():
            for copy in backward:
                getattr(copy, action)()

    def swap(send, recv, slot, k, back=False):
        part = groups[k]

        def body(i, carry):
            to = lax.rem(e + i, NE)
            copy = pltpu.make_async_remote_copy(
                send.at[part, to], recv.at[part, e], swap_send.at[slot], swap_recv.at[slot],
                device_id=(to, s), device_id_type=MESH,
            )
            if k == 0 or back:
                copy.start()
            else:
                nothing = (first & (to < HALF)) | (last & (to >= HALF))

                @pl.when(jnp.logical_not(nothing))
                def _():
                    copy.start()

            return carry

        def run():
            lax.fori_loop(1, NE, body, 0)
            own = pltpu.make_async_copy(send.at[part, e], recv.at[part, e], swap_recv.at[slot])
            own.start()

        if k == 0:
            run()
        elif back:
            pl.when(jnp.logical_not(idle))(run)
        else:
            lax.fori_loop(1, NE, body, 0)

            @pl.when(jnp.logical_not(idle))
            def _():
                pltpu.make_async_copy(
                    send.at[part, e], recv.at[part, e], swap_recv.at[slot]
                ).start()

    def finish(ref, sem, count, k):
        full = ref.at[groups[k], pl.ds(0, count)]
        pltpu.make_async_copy(full, full, sem).wait()

    def wait_swap(recv, slot, k, back=False):
        sem = swap_recv.at[slot]
        if k == 0:
            finish(recv, sem, NE, k)
        elif back:
            ends = first | last
            pl.when(ends)(lambda: finish(recv, sem, HALF, k))
            pl.when(jnp.logical_not(ends))(lambda: finish(recv, sem, NE, k))
        else:
            pl.when(jnp.logical_not(idle))(lambda: finish(recv, sem, NE, k))

    def wait_sent(send, slot, k, back=False):
        sem = swap_send.at[slot]
        if k == 0:
            finish(send, sem, NE - 1, k)
        elif back:
            pl.when(jnp.logical_not(idle))(lambda: finish(send, sem, NE - 1, k))
        else:
            ends = first | last
            pl.when(jnp.logical_not(ends))(lambda: finish(send, sem, NE - 1, k))
            pl.when(idle)(lambda: finish(send, sem, HALF, k))
            pl.when(ends & jnp.logical_not(idle))(lambda: finish(send, sem, HALF - 1, k))

    members = ((1, 2), (0,))
    edges([w_next, p_next], [w_prev, p_prev], "start")
    for k in range(2):
        for c in members[k]:
            for half in range(2):
                band = c if half == 0 else 2 - c
                re = g4[1 + half, band, 0].astype(F32)
                im = g4[1 + half, band, 1].astype(F32)
                g_send[c, pl.ds(half * HALF, HALF)] = pack(re, im).astype(BF16)
        swap(g_send, g_recv, k, k)

    @pl.when(idle)
    def _():
        g_recv[0] = jnp.zeros(g_recv.shape[1:], BF16)
        s_recv[0] = jnp.zeros(s_recv.shape[1:], BF16)

    edges([w_next, p_next], [w_prev, p_prev], "wait_recv")
    firsts = [products_row(w4, p4, 1 + half) for half in range(2)]
    for k in range(2):
        for c in members[k]:
            for half in range(2):
                band = c if half == 0 else 2 - c
                block = close_row(firsts[half], w4, 1 + half, band)
                s_send[c, pl.ds(half * HALF, HALF)] = pack(block[:, :B], block[:, B:]).astype(BF16)
        swap(s_send, s_recv, 2 + k, k)
    edges([g_next], [g_prev], "start")

    def spectrum(recv, c):
        stage[...] = recv[c].astype(F32).reshape(NE * 8, B)
        rows = [stage[pl.ds(r, NE, stride=8), :].astype(BF16) for r in range(8)]
        data = jnp.concatenate(
            [jnp.concatenate(rows[:4], axis=1), jnp.concatenate(rows[4:], axis=1)], axis=0
        )
        return dot(fwd_ref[...], jnp.concatenate([data, data], axis=0))

    for load in table_loads:
        load.wait()
    for k in range(2):
        wait_swap(g_recv, k, k)
        for c in members[k]:
            g_spec[c] = spectrum(g_recv, c)
    for k in range(2):
        wait_swap(s_recv, 2 + k, k)
        for c in members[k]:
            spec = spectrum(s_recv, c)
            sr, si = spec[: 2 * NE], spec[2 * NE :]
            gr, gi = g_spec[c, : 2 * NE], g_spec[c, 2 * NE :]
            both = jnp.concatenate([gr * sr - gi * si, gr * si + gi * sr], axis=0)
            upper = both.astype(BF16)
            lower = (both - upper.astype(F32)).astype(BF16)
            sums = dot(back_ref[...], jnp.concatenate([upper, lower, upper], axis=0))
            for r in range(4):
                stage[pl.ds(r, NE, stride=8), :] = sums[:NE, r * B : (r + 1) * B]
                stage[pl.ds(r + 4, NE, stride=8), :] = sums[NE:, r * B : (r + 1) * B]
            c_send[c] = stage[...].reshape(NE, 8, B).astype(BF16)
        swap(c_send, c_recv, 4 + k, k, back=True)
    edges([g_next], [g_prev], "wait_recv")

    def place(packed, row, band):
        re, im = unpack(packed.astype(F32))
        s4[row, band, 0] = re.astype(BF16)
        s4[row, band, 1] = im.astype(BF16)

    for k in range(2):
        wait_swap(c_recv, 4 + k, k, back=True)
        edges(c_nexts[k : k + 1], c_prevs[k : k + 1], "start")
        for c in members[k]:
            place(c_recv[c, pl.ds(0, HALF)], 1, c)
            place(c_recv[c, pl.ds(HALF, HALF)], 2, 2 - c)
    for k in range(2):
        edges(c_nexts[k : k + 1], c_prevs[k : k + 1], "wait_recv")
        for c in members[k]:
            place(c_prev[c], 0, 2 - c)
            place(c_next[c], 3, c)
    for half in range(2):
        products = products_row(g4, s4, 1 + half)
        for band in range(3):
            block = close_row(products, g4, 1 + half, band)
            out_ref[half, band, 0] = block[:, :B].astype(BF16)
            out_ref[half, band, 1] = block[:, B:].astype(BF16)

    edges([w_next, p_next, g_next, *c_nexts], [w_prev, p_prev, g_prev, *c_prevs], "wait_send")
    for k in range(2):
        wait_sent(g_send, k, k)
        wait_sent(s_send, 2 + k, k)
        wait_sent(c_send, 4 + k, k, back=True)


def local(screening, polarization, propagator):
    fwd, back = tables((3.0 * B / NE) ** 0.5)
    four = pltpu.VMEM((4, 3, 2, B, B), BF16)
    full = pltpu.VMEM((3, NE, 8, B), BF16)
    rim = pltpu.VMEM((3, HALF, 8, B), BF16)
    hbm = pl.BlockSpec(memory_space=pltpu.HBM)
    vmem = pl.BlockSpec(memory_space=pltpu.VMEM)
    out = pl.pallas_call(
        kernel,
        name="self_energy",
        out_shape=jax.ShapeDtypeStruct((2, 3, 2, B, B), BF16),
        in_specs=[hbm, hbm, hbm, hbm, hbm],
        out_specs=vmem,
        scratch_shapes=[
            four, four, four, four,
            full, full, full, full, full, full, rim, rim,
            pltpu.VMEM(fwd.shape, BF16),
            pltpu.VMEM(back.shape, BF16),
            pltpu.VMEM((3, 4 * NE, 4 * B), F32),
            pltpu.VMEM((NE * 8, B), F32),
            pltpu.SemaphoreType.DMA((5,)),
            pltpu.SemaphoreType.DMA((10,)),
            pltpu.SemaphoreType.DMA((10,)),
            pltpu.SemaphoreType.DMA((6,)),
            pltpu.SemaphoreType.DMA((6,)),
        ],
        compiler_params=pltpu.CompilerParams(
            collective_id=0, has_side_effects=True, vmem_limit_bytes=62 << 20
        ),
    )(screening[0], polarization[0], propagator[0], jnp.asarray(fwd), jnp.asarray(back))
    return out[None]


def solution(mesh):
    spec = P("energy", "space", None, None, None, None)
    return jax.shard_map(
        local, mesh=mesh, in_specs=(spec, spec, spec), out_specs=spec, check_vma=False
    )
```

```python
import math

import jax
import jax.numpy as jnp
import ml_dtypes
import numpy as np
from jax import lax
from jax.experimental import pallas as pl
from jax.experimental.pallas import tpu as pltpu
from jax.sharding import PartitionSpec as P

MESH = pl.DeviceIdType.MESH
B = 128
NE = 64
NS = 4
HALF = NE // 2
F32 = jnp.float32
BF16 = jnp.bfloat16


def split_np(table):
    upper = table.astype(ml_dtypes.bfloat16)
    lower = (table - upper.astype(np.float64)).astype(ml_dtypes.bfloat16)
    return upper, lower


def tables(factor):
    freq = np.arange(2 * NE)
    time = np.arange(NE)
    angle = (freq[:, None] * time[None, :] % (2 * NE)) * (math.pi / NE)
    cos, sin = np.cos(angle), np.sin(angle)
    fwd = np.block([[cos, sin], [-sin, cos]])
    back = np.block([[cos.T, -sin.T], [sin.T, cos.T]]) * (factor / (2 * NE))
    fh, fl = split_np(fwd)
    bh, bl = split_np(back)
    return np.concatenate([fh, fl], 1), np.concatenate([bh, bh, bl], 1)


def dot(a, b):
    return jnp.dot(a, b, preferred_element_type=F32)


def dot_nt(a, b):
    return lax.dot_general(a, b, (((1,), (1,)), ((), ())), preferred_element_type=F32)


def wide(ref, row, band):
    return jnp.concatenate([ref[row, band, 0], ref[row, band, 1]], axis=1)


def embed(ref, row, band):
    re, im = ref[row, band, 0], ref[row, band, 1]
    return jnp.concatenate(
        [jnp.concatenate([re, im], axis=1), jnp.concatenate([-im, re], axis=1)], axis=0
    )


def products_row(outer, inner, row):
    products = {}
    for offset in range(-2, 3):
        steps = [k for k in (-1, 0, 1) if abs(offset - k) <= 1]
        lhs = jnp.concatenate([wide(outer, row, k + 1) for k in steps], axis=1)
        rhs = jnp.concatenate([embed(inner, row + k, offset - k + 1) for k in steps], axis=0)
        products[offset] = dot(lhs, rhs).astype(BF16)
    return products


def close_row(products, outer, row, band):
    offsets = range(band - 2, band + 1)
    lhs = jnp.concatenate([products[d] for d in offsets], axis=1)
    rhs = jnp.concatenate([embed(outer, row + band - 1, d - band + 2) for d in offsets], axis=1)
    return dot_nt(lhs, rhs)


def pack(re, im):
    re, im = re.reshape(16, 8, B), im.reshape(16, 8, B)
    low = lax.broadcasted_iota(jnp.int32, (16, 8, B), 1) < 4
    even = jnp.where(low, re, pltpu.roll(im, 4, 1))
    odd = jnp.where(low, pltpu.roll(re, 4, 1), im)
    return jnp.stack([even, odd], axis=1).reshape(HALF, 8, B)


def unpack(packed):
    pairs = packed.reshape(16, 2, 8, B)
    even, odd = pairs[:, 0], pairs[:, 1]
    low = lax.broadcasted_iota(jnp.int32, (16, 8, B), 1) < 4
    re = jnp.where(low, even, pltpu.roll(odd, 4, 1))
    im = jnp.where(low, pltpu.roll(even, 4, 1), odd)
    return re.reshape(B, B), im.reshape(B, B)


def kernel(
    w_hbm, p_hbm, g_hbm, fwd_hbm, back_hbm, out_ref,
    w4, p4, g4, s4, g_send, g_recv, s_send, s_recv, c_send, c_recv, c_prev, c_next,
    fwd_ref, back_ref, g_spec, stage, load_sem, edge_send, edge_recv, swap_send, swap_recv,
):
    e = lax.axis_index("energy")
    s = lax.axis_index("space")
    barrier = pltpu.get_barrier_semaphore()
    loads = [
        pltpu.make_async_copy(src, dst.at[pl.ds(1, 2)], load_sem.at[i])
        for i, (src, dst) in enumerate(((g_hbm, g4), (w_hbm, w4), (p_hbm, p4)))
    ]
    table_loads = [
        pltpu.make_async_copy(fwd_hbm, fwd_ref, load_sem.at[3]),
        pltpu.make_async_copy(back_hbm, back_ref, load_sem.at[4]),
    ]
    for load in loads + table_loads:
        load.start()

    def greet(i, carry):
        pl.semaphore_signal(barrier, inc=1, device_id=(lax.rem(e + i, NE), s), device_id_type=MESH)
        return carry

    @pl.when(s > 0)
    def _():
        pl.semaphore_signal(barrier, inc=1, device_id=(e, s - 1), device_id_type=MESH)

    @pl.when(s < NS - 1)
    def _():
        pl.semaphore_signal(barrier, inc=1, device_id=(e, s + 1), device_id_type=MESH)

    lax.fori_loop(1, NE, greet, 0)

    first, last = s == 0, s == NS - 1
    low = e < HALF
    idle = (first & low) | (last & jnp.logical_not(low))
    for load in loads:
        load.wait()

    @pl.when(first)
    def _():
        for ref in (w4, p4, g4):
            ref[0] = jnp.zeros(ref.shape[1:], BF16)
            ref[1, 0] = jnp.zeros(ref.shape[2:], BF16)
        c_prev[...] = jnp.zeros(c_prev.shape, BF16)
        c_recv[0, :HALF] = jnp.zeros((HALF, 8, B), BF16)

    @pl.when(last)
    def _():
        for ref in (w4, p4, g4):
            ref[3] = jnp.zeros(ref.shape[1:], BF16)
            ref[2, 2] = jnp.zeros(ref.shape[2:], BF16)
        c_next[...] = jnp.zeros(c_next.shape, BF16)
        c_recv[0, HALF:] = jnp.zeros((HALF, 8, B), BF16)

    pl.semaphore_wait(barrier, NE - 1 + (s > 0).astype(jnp.int32) + (s < NS - 1).astype(jnp.int32))

    def to_next(src, dst, i):
        return pltpu.make_async_remote_copy(
            src, dst, edge_send.at[i], edge_recv.at[i], device_id=(e, s + 1), device_id_type=MESH
        )

    def to_prev(src, dst, i):
        return pltpu.make_async_remote_copy(
            src, dst, edge_send.at[i], edge_recv.at[i], device_id=(e, s - 1), device_id_type=MESH
        )

    groups = (pl.ds(1, 2), pl.ds(0, 1))
    w_next, w_prev = to_next(w4.at[2], w4.at[0], 0), to_prev(w4.at[1], w4.at[3], 1)
    p_next, p_prev = to_next(p4.at[2], p4.at[0], 2), to_prev(p4.at[1], p4.at[3], 3)
    g_next, g_prev = to_next(g4.at[2], g4.at[0], 4), to_prev(g4.at[1], g4.at[3], 5)
    c_nexts = [
        to_next(c_recv.at[part, pl.ds(HALF, HALF)], c_prev.at[part], 6 + k)
        for k, part in enumerate(groups)
    ]
    c_prevs = [
        to_prev(c_recv.at[part, pl.ds(0, HALF)], c_next.at[part], 8 + k)
        for k, part in enumerate(groups)
    ]

    def edges(nexts, prevs, action):
        forward, backward = (prevs, nexts) if action == "wait_recv" else (nexts, prevs)

        @pl.when(s < NS - 1)
        def _():
            for copy in forward:
                getattr(copy, action)()

        @pl.when(s > 0)
        def _():
            for copy in backward:
                getattr(copy, action)()

    def swap(send, recv, slot, k, back=False):
        part = groups[k]

        def body(i, carry):
            to = lax.rem(e + i, NE)
            copy = pltpu.make_async_remote_copy(
                send.at[part, to], recv.at[part, e], swap_send.at[slot], swap_recv.at[slot],
                device_id=(to, s), device_id_type=MESH,
            )
            if k == 0 or back:
                copy.start()
            else:
                nothing = (first & (to < HALF)) | (last & (to >= HALF))

                @pl.when(jnp.logical_not(nothing))
                def _():
                    copy.start()

            return carry

        def run():
            lax.fori_loop(1, NE, body, 0)
            own = pltpu.make_async_copy(send.at[part, e], recv.at[part, e], swap_recv.at[slot])
            own.start()

        if k == 0:
            run()
        elif back:
            pl.when(jnp.logical_not(idle))(run)
        else:
            lax.fori_loop(1, NE, body, 0)

            @pl.when(jnp.logical_not(idle))
            def _():
                pltpu.make_async_copy(
                    send.at[part, e], recv.at[part, e], swap_recv.at[slot]
                ).start()

    def swap_all(send, recv, slot):
        def copy(part, to):
            return pltpu.make_async_remote_copy(
                send.at[part, to], recv.at[part, e], swap_send.at[slot], swap_recv.at[slot],
                device_id=(to, s), device_id_type=MESH,
            )

        def body(i, carry):
            to = lax.rem(e + i, NE)
            nothing = (first & (to < HALF)) | (last & (to >= HALF))

            @pl.when(nothing)
            def _():
                copy(pl.ds(1, 2), to).start()

            @pl.when(jnp.logical_not(nothing))
            def _():
                copy(pl.ds(0, 3), to).start()

            return carry

        lax.fori_loop(1, NE, body, 0)

        @pl.when(idle)
        def _():
            own = pl.ds(1, 2)
            pltpu.make_async_copy(send.at[own, e], recv.at[own, e], swap_recv.at[slot]).start()

        @pl.when(jnp.logical_not(idle))
        def _():
            pltpu.make_async_copy(send.at[:, e], recv.at[:, e], swap_recv.at[slot]).start()

    def wait_all(recv, slot):
        sem = swap_recv.at[slot]

        @pl.when(idle)
        def _():
            pltpu.make_async_copy(recv.at[pl.ds(1, 2)], recv.at[pl.ds(1, 2)], sem).wait()

        @pl.when(jnp.logical_not(idle))
        def _():
            pltpu.make_async_copy(recv, recv, sem).wait()

    def wait_all_sent(send, slot):
        sem = swap_send.at[slot]
        pair = send.at[pl.ds(1, 2), pl.ds(0, NE - 1)]
        pltpu.make_async_copy(pair, pair, sem).wait()
        ends = first | last
        pl.when(jnp.logical_not(ends))(lambda: finish(send, sem, NE - 1, 1))
        pl.when(idle)(lambda: finish(send, sem, HALF, 1))
        pl.when(ends & jnp.logical_not(idle))(lambda: finish(send, sem, HALF - 1, 1))

    def finish(ref, sem, count, k):
        full = ref.at[groups[k], pl.ds(0, count)]
        pltpu.make_async_copy(full, full, sem).wait()

    def wait_swap(recv, slot, k, back=False):
        sem = swap_recv.at[slot]
        if k == 0:
            finish(recv, sem, NE, k)
        elif back:
            ends = first | last
            pl.when(ends)(lambda: finish(recv, sem, HALF, k))
            pl.when(jnp.logical_not(ends))(lambda: finish(recv, sem, NE, k))
        else:
            pl.when(jnp.logical_not(idle))(lambda: finish(recv, sem, NE, k))

    def wait_sent(send, slot, k, back=False):
        sem = swap_send.at[slot]
        if k == 0:
            finish(send, sem, NE - 1, k)
        elif back:
            pl.when(jnp.logical_not(idle))(lambda: finish(send, sem, NE - 1, k))
        else:
            ends = first | last
            pl.when(jnp.logical_not(ends))(lambda: finish(send, sem, NE - 1, k))
            pl.when(idle)(lambda: finish(send, sem, HALF, k))
            pl.when(ends & jnp.logical_not(idle))(lambda: finish(send, sem, HALF - 1, k))

    members = ((1, 2), (0,))
    edges([w_next, p_next], [w_prev, p_prev], "start")
    for c in range(3):
        for half in range(2):
            band = c if half == 0 else 2 - c
            re = g4[1 + half, band, 0].astype(F32)
            im = g4[1 + half, band, 1].astype(F32)
            g_send[c, pl.ds(half * HALF, HALF)] = pack(re, im).astype(BF16)
    @pl.when(jnp.logical_not(first | last))
    def _():
        swap_all(g_send, g_recv, 0)


    @pl.when(idle)
    def _():
        g_recv[0] = jnp.zeros(g_recv.shape[1:], BF16)
        s_recv[0] = jnp.zeros(s_recv.shape[1:], BF16)

    edges([w_next, p_next], [w_prev, p_prev], "wait_recv")
    firsts = [products_row(w4, p4, 1 + half) for half in range(2)]
    for k in range(2):
        for c in members[k]:
            for half in range(2):
                band = c if half == 0 else 2 - c
                block = close_row(firsts[half], w4, 1 + half, band)
                s_send[c, pl.ds(half * HALF, HALF)] = pack(block[:, :B], block[:, B:]).astype(BF16)
        swap(s_send, s_recv, 2 + k, k)
    @pl.when(first | last)
    def _():
        swap_all(g_send, g_recv, 0)

    edges([g_next], [g_prev], "start")

    def spectrum(recv, c):
        stage[...] = recv[c].astype(F32).reshape(NE * 8, B)
        rows = [stage[pl.ds(r, NE, stride=8), :].astype(BF16) for r in range(8)]
        data = jnp.concatenate(
            [jnp.concatenate(rows[:4], axis=1), jnp.concatenate(rows[4:], axis=1)], axis=0
        )
        return dot(fwd_ref[...], jnp.concatenate([data, data], axis=0))

    for load in table_loads:
        load.wait()
    wait_all(g_recv, 0)
    for c in range(3):
        g_spec[c] = spectrum(g_recv, c)
    for k in range(2):
        wait_swap(s_recv, 2 + k, k)
        for c in members[k]:
            spec = spectrum(s_recv, c)
            sr, si = spec[: 2 * NE], spec[2 * NE :]
            gr, gi = g_spec[c, : 2 * NE], g_spec[c, 2 * NE :]
            both = jnp.concatenate([gr * sr - gi * si, gr * si + gi * sr], axis=0)
            upper = both.astype(BF16)
            lower = (both - upper.astype(F32)).astype(BF16)
            sums = dot(back_ref[...], jnp.concatenate([upper, lower, upper], axis=0))
            for r in range(4):
                stage[pl.ds(r, NE, stride=8), :] = sums[:NE, r * B : (r + 1) * B]
                stage[pl.ds(r + 4, NE, stride=8), :] = sums[NE:, r * B : (r + 1) * B]
            c_send[c] = stage[...].reshape(NE, 8, B).astype(BF16)
        swap(c_send, c_recv, 4 + k, k, back=True)
    edges([g_next], [g_prev], "wait_recv")

    def place(packed, row, band):
        re, im = unpack(packed.astype(F32))
        s4[row, band, 0] = re.astype(BF16)
        s4[row, band, 1] = im.astype(BF16)

    for k in range(2):
        wait_swap(c_recv, 4 + k, k, back=True)
        edges(c_nexts[k : k + 1], c_prevs[k : k + 1], "start")
        for c in members[k]:
            place(c_recv[c, pl.ds(0, HALF)], 1, c)
            place(c_recv[c, pl.ds(HALF, HALF)], 2, 2 - c)
    for k in range(2):
        edges(c_nexts[k : k + 1], c_prevs[k : k + 1], "wait_recv")
        for c in members[k]:
            place(c_prev[c], 0, 2 - c)
            place(c_next[c], 3, c)
    for half in range(2):
        products = products_row(g4, s4, 1 + half)
        for band in range(3):
            block = close_row(products, g4, 1 + half, band)
            out_ref[half, band, 0] = block[:, :B].astype(BF16)
            out_ref[half, band, 1] = block[:, B:].astype(BF16)

    edges([w_next, p_next, g_next, *c_nexts], [w_prev, p_prev, g_prev, *c_prevs], "wait_send")
    wait_all_sent(g_send, 0)
    for k in range(2):
        wait_sent(s_send, 2 + k, k)
        wait_sent(c_send, 4 + k, k, back=True)


def local(screening, polarization, propagator):
    fwd, back = tables((3.0 * B / NE) ** 0.5)
    four = pltpu.VMEM((4, 3, 2, B, B), BF16)
    full = pltpu.VMEM((3, NE, 8, B), BF16)
    rim = pltpu.VMEM((3, HALF, 8, B), BF16)
    hbm = pl.BlockSpec(memory_space=pltpu.HBM)
    vmem = pl.BlockSpec(memory_space=pltpu.VMEM)
    out = pl.pallas_call(
        kernel,
        name="self_energy",
        out_shape=jax.ShapeDtypeStruct((2, 3, 2, B, B), BF16),
        in_specs=[hbm, hbm, hbm, hbm, hbm],
        out_specs=vmem,
        scratch_shapes=[
            four, four, four, four,
            full, full, full, full, full, full, rim, rim,
            pltpu.VMEM(fwd.shape, BF16),
            pltpu.VMEM(back.shape, BF16),
            pltpu.VMEM((3, 4 * NE, 4 * B), F32),
            pltpu.VMEM((NE * 8, B), F32),
            pltpu.SemaphoreType.DMA((5,)),
            pltpu.SemaphoreType.DMA((10,)),
            pltpu.SemaphoreType.DMA((10,)),
            pltpu.SemaphoreType.DMA((6,)),
            pltpu.SemaphoreType.DMA((6,)),
        ],
        compiler_params=pltpu.CompilerParams(
            collective_id=0, has_side_effects=True, vmem_limit_bytes=62 << 20
        ),
    )(screening[0], polarization[0], propagator[0], jnp.asarray(fwd), jnp.asarray(back))
    return out[None]


def solution(mesh):
    spec = P("energy", "space", None, None, None, None)
    return jax.shard_map(
        local, mesh=mesh, in_specs=(spec, spec, spec), out_specs=spec, check_vma=False
    )
```

```python
import math

import jax
import jax.numpy as jnp
import ml_dtypes
import numpy as np
from jax import lax
from jax.experimental import pallas as pl
from jax.experimental.pallas import tpu as pltpu
from jax.sharding import PartitionSpec as P

MESH = pl.DeviceIdType.MESH
B = 128
NE = 64
NS = 4
HALF = NE // 2
F32 = jnp.float32
BF16 = jnp.bfloat16


def split_np(table):
    upper = table.astype(ml_dtypes.bfloat16)
    lower = (table - upper.astype(np.float64)).astype(ml_dtypes.bfloat16)
    return upper, lower


def tables(factor):
    freq = np.arange(2 * NE)
    time = np.arange(NE)
    angle = (freq[:, None] * time[None, :] % (2 * NE)) * (math.pi / NE)
    cos, sin = np.cos(angle), np.sin(angle)
    fwd = np.block([[cos, sin], [-sin, cos]])
    back = np.block([[cos.T, -sin.T], [sin.T, cos.T]]) * (factor / (2 * NE))
    fh, fl = split_np(fwd)
    bh, bl = split_np(back)
    table = np.zeros((8 * B, 2 * B), ml_dtypes.bfloat16)
    table[: 5 * B] = np.concatenate([np.concatenate([fh, fl], 1), bh, bh, bl], 0)
    return table


def dot(a, b):
    return jnp.dot(a, b, preferred_element_type=F32)


def dot_nt(a, b):
    return lax.dot_general(a, b, (((1,), (1,)), ((), ())), preferred_element_type=F32)


def wide(ref, row, band):
    return jnp.concatenate([ref[row, band, 0], ref[row, band, 1]], axis=1)


def embed(ref, row, band):
    re, im = ref[row, band, 0], ref[row, band, 1]
    return jnp.concatenate(
        [jnp.concatenate([re, im], axis=1), jnp.concatenate([-im, re], axis=1)], axis=0
    )


def products_row(outer, inner, row):
    products = {}
    for offset in range(-2, 3):
        steps = [k for k in (-1, 0, 1) if abs(offset - k) <= 1]
        lhs = jnp.concatenate([wide(outer, row, k + 1) for k in steps], axis=1)
        rhs = jnp.concatenate([embed(inner, row + k, offset - k + 1) for k in steps], axis=0)
        products[offset] = dot(lhs, rhs).astype(BF16)
    return products


def close_row(products, outer, row, band):
    offsets = range(band - 2, band + 1)
    lhs = jnp.concatenate([products[d] for d in offsets], axis=1)
    rhs = jnp.concatenate([embed(outer, row + band - 1, d - band + 2) for d in offsets], axis=1)
    return dot_nt(lhs, rhs)


def pack(re, im):
    re, im = re.reshape(16, 8, B), im.reshape(16, 8, B)
    low = lax.broadcasted_iota(jnp.int32, (16, 8, B), 1) < 4
    even = jnp.where(low, re, pltpu.roll(im, 4, 1))
    odd = jnp.where(low, pltpu.roll(re, 4, 1), im)
    return jnp.stack([even, odd], axis=1).reshape(HALF, 8, B)


def unpack(packed):
    pairs = packed.reshape(16, 2, 8, B)
    even, odd = pairs[:, 0], pairs[:, 1]
    low = lax.broadcasted_iota(jnp.int32, (16, 8, B), 1) < 4
    re = jnp.where(low, even, pltpu.roll(odd, 4, 1))
    im = jnp.where(low, pltpu.roll(even, 4, 1), odd)
    return re.reshape(B, B), im.reshape(B, B)


def kernel(
    w_hbm, p_hbm, g_hbm, table_hbm, out_ref,
    w4, p4, g4, s4, g_send, g_recv, s_send, s_recv, c_send, c_recv, c_prev, c_next,
    table, g_spec, stage, load_sem, edge_send, edge_recv, swap_send, swap_recv,
):
    e = lax.axis_index("energy")
    s = lax.axis_index("space")
    barrier = pltpu.get_barrier_semaphore()
    loads = [
        pltpu.make_async_copy(src, dst.at[pl.ds(1, 2)], load_sem.at[i])
        for i, (src, dst) in enumerate(((g_hbm, g4), (w_hbm, w4), (p_hbm, p4)))
    ]
    table_loads = [
        pltpu.make_async_copy(table_hbm.at[pl.ds(0, 5 * B)], table, load_sem.at[3]),
    ]
    for load in loads + table_loads:
        load.start()

    def greet(i, carry):
        pl.semaphore_signal(barrier, inc=1, device_id=(lax.rem(e + i, NE), s), device_id_type=MESH)
        return carry

    @pl.when(s > 0)
    def _():
        pl.semaphore_signal(barrier, inc=1, device_id=(e, s - 1), device_id_type=MESH)

    @pl.when(s < NS - 1)
    def _():
        pl.semaphore_signal(barrier, inc=1, device_id=(e, s + 1), device_id_type=MESH)

    lax.fori_loop(1, NE, greet, 0)

    first, last = s == 0, s == NS - 1
    low = e < HALF
    idle = (first & low) | (last & jnp.logical_not(low))
    for load in loads:
        load.wait()

    @pl.when(first)
    def _():
        for ref in (w4, p4, g4):
            ref[0] = jnp.zeros(ref.shape[1:], BF16)
            ref[1, 0] = jnp.zeros(ref.shape[2:], BF16)
        c_prev[...] = jnp.zeros(c_prev.shape, BF16)
        c_recv[0, :HALF] = jnp.zeros((HALF, 8, B), BF16)

    @pl.when(last)
    def _():
        for ref in (w4, p4, g4):
            ref[3] = jnp.zeros(ref.shape[1:], BF16)
            ref[2, 2] = jnp.zeros(ref.shape[2:], BF16)
        c_next[...] = jnp.zeros(c_next.shape, BF16)
        c_recv[0, HALF:] = jnp.zeros((HALF, 8, B), BF16)

    pl.semaphore_wait(barrier, NE - 1 + (s > 0).astype(jnp.int32) + (s < NS - 1).astype(jnp.int32))

    def to_next(src, dst, i):
        return pltpu.make_async_remote_copy(
            src, dst, edge_send.at[i], edge_recv.at[i], device_id=(e, s + 1), device_id_type=MESH
        )

    def to_prev(src, dst, i):
        return pltpu.make_async_remote_copy(
            src, dst, edge_send.at[i], edge_recv.at[i], device_id=(e, s - 1), device_id_type=MESH
        )

    groups = (pl.ds(1, 2), pl.ds(0, 1))
    w_next, w_prev = to_next(w4.at[2], w4.at[0], 0), to_prev(w4.at[1], w4.at[3], 1)
    p_next, p_prev = to_next(p4.at[2], p4.at[0], 2), to_prev(p4.at[1], p4.at[3], 3)
    g_next, g_prev = to_next(g4.at[2], g4.at[0], 4), to_prev(g4.at[1], g4.at[3], 5)
    c_nexts = [
        to_next(c_recv.at[part, pl.ds(HALF, HALF)], c_prev.at[part], 6 + k)
        for k, part in enumerate(groups)
    ]
    c_prevs = [
        to_prev(c_recv.at[part, pl.ds(0, HALF)], c_next.at[part], 8 + k)
        for k, part in enumerate(groups)
    ]

    def edges(nexts, prevs, action):
        forward, backward = (prevs, nexts) if action == "wait_recv" else (nexts, prevs)

        @pl.when(s < NS - 1)
        def _():
            for copy in forward:
                getattr(copy, action)()

        @pl.when(s > 0)
        def _():
            for copy in backward:
                getattr(copy, action)()

    def swap(send, recv, slot, k, back=False):
        part = groups[k]

        def body(i, carry):
            to = lax.rem(e + i, NE)
            copy = pltpu.make_async_remote_copy(
                send.at[part, to], recv.at[part, e], swap_send.at[slot], swap_recv.at[slot],
                device_id=(to, s), device_id_type=MESH,
            )
            if k == 0 or back:
                copy.start()
            else:
                nothing = (first & (to < HALF)) | (last & (to >= HALF))

                @pl.when(jnp.logical_not(nothing))
                def _():
                    copy.start()

            return carry

        def run():
            lax.fori_loop(1, NE, body, 0)
            own = pltpu.make_async_copy(send.at[part, e], recv.at[part, e], swap_recv.at[slot])
            own.start()

        if k == 0:
            run()
        elif back:
            pl.when(jnp.logical_not(idle))(run)
        else:
            lax.fori_loop(1, NE, body, 0)

            @pl.when(jnp.logical_not(idle))
            def _():
                pltpu.make_async_copy(
                    send.at[part, e], recv.at[part, e], swap_recv.at[slot]
                ).start()

    def swap_all(send, recv, slot):
        def copy(part, to):
            return pltpu.make_async_remote_copy(
                send.at[part, to], recv.at[part, e], swap_send.at[slot], swap_recv.at[slot],
                device_id=(to, s), device_id_type=MESH,
            )

        def body(i, carry):
            to = lax.rem(e + i, NE)
            nothing = (first & (to < HALF)) | (last & (to >= HALF))

            @pl.when(nothing)
            def _():
                copy(pl.ds(1, 2), to).start()

            @pl.when(jnp.logical_not(nothing))
            def _():
                copy(pl.ds(0, 3), to).start()

            return carry

        lax.fori_loop(1, NE, body, 0)

        @pl.when(idle)
        def _():
            own = pl.ds(1, 2)
            pltpu.make_async_copy(send.at[own, e], recv.at[own, e], swap_recv.at[slot]).start()

        @pl.when(jnp.logical_not(idle))
        def _():
            pltpu.make_async_copy(send.at[:, e], recv.at[:, e], swap_recv.at[slot]).start()

    def wait_all(recv, slot):
        sem = swap_recv.at[slot]

        @pl.when(idle)
        def _():
            pltpu.make_async_copy(recv.at[pl.ds(1, 2)], recv.at[pl.ds(1, 2)], sem).wait()

        @pl.when(jnp.logical_not(idle))
        def _():
            pltpu.make_async_copy(recv, recv, sem).wait()

    def wait_all_sent(send, slot):
        sem = swap_send.at[slot]
        pair = send.at[pl.ds(1, 2), pl.ds(0, NE - 1)]
        pltpu.make_async_copy(pair, pair, sem).wait()
        ends = first | last
        pl.when(jnp.logical_not(ends))(lambda: finish(send, sem, NE - 1, 1))
        pl.when(idle)(lambda: finish(send, sem, HALF, 1))
        pl.when(ends & jnp.logical_not(idle))(lambda: finish(send, sem, HALF - 1, 1))

    def finish(ref, sem, count, k):
        full = ref.at[groups[k], pl.ds(0, count)]
        pltpu.make_async_copy(full, full, sem).wait()

    def wait_swap(recv, slot, k, back=False):
        sem = swap_recv.at[slot]
        if k == 0:
            finish(recv, sem, NE, k)
        elif back:
            ends = first | last
            pl.when(ends)(lambda: finish(recv, sem, HALF, k))
            pl.when(jnp.logical_not(ends))(lambda: finish(recv, sem, NE, k))
        else:
            pl.when(jnp.logical_not(idle))(lambda: finish(recv, sem, NE, k))

    def wait_sent(send, slot, k, back=False):
        sem = swap_send.at[slot]
        if k == 0:
            finish(send, sem, NE - 1, k)
        elif back:
            pl.when(jnp.logical_not(idle))(lambda: finish(send, sem, NE - 1, k))
        else:
            ends = first | last
            pl.when(jnp.logical_not(ends))(lambda: finish(send, sem, NE - 1, k))
            pl.when(idle)(lambda: finish(send, sem, HALF, k))
            pl.when(ends & jnp.logical_not(idle))(lambda: finish(send, sem, HALF - 1, k))

    members = ((1, 2), (0,))
    edges([w_next, p_next], [w_prev, p_prev], "start")
    for c in range(3):
        for half in range(2):
            band = c if half == 0 else 2 - c
            re = g4[1 + half, band, 0].astype(F32)
            im = g4[1 + half, band, 1].astype(F32)
            g_send[c, pl.ds(half * HALF, HALF)] = pack(re, im).astype(BF16)
    @pl.when(jnp.logical_not(first | last))
    def _():
        swap_all(g_send, g_recv, 0)


    @pl.when(idle)
    def _():
        g_recv[0] = jnp.zeros(g_recv.shape[1:], BF16)
        s_recv[0] = jnp.zeros(s_recv.shape[1:], BF16)

    edges([w_next, p_next], [w_prev, p_prev], "wait_recv")
    firsts = [products_row(w4, p4, 1 + half) for half in range(2)]
    for k in range(2):
        for c in members[k]:
            for half in range(2):
                band = c if half == 0 else 2 - c
                block = close_row(firsts[half], w4, 1 + half, band)
                s_send[c, pl.ds(half * HALF, HALF)] = pack(block[:, :B], block[:, B:]).astype(BF16)
        swap(s_send, s_recv, 2 + k, k)
    @pl.when(first | last)
    def _():
        swap_all(g_send, g_recv, 0)

    edges([g_next], [g_prev], "start")

    def spectrum(recv, c):
        stage[...] = recv[c].astype(F32).reshape(NE * 8, B)
        rows = [stage[pl.ds(r, NE, stride=8), :].astype(BF16) for r in range(8)]
        data = jnp.concatenate(
            [jnp.concatenate(rows[:4], axis=1), jnp.concatenate(rows[4:], axis=1)], axis=0
        )
        return dot(table[: 2 * B], jnp.concatenate([data, data], axis=0))

    for load in table_loads:
        load.wait()
    wait_all(g_recv, 0)
    for c in range(3):
        g_spec[c] = spectrum(g_recv, c)
    for k in range(2):
        wait_swap(s_recv, 2 + k, k)
        for c in members[k]:
            spec = spectrum(s_recv, c)
            sr, si = spec[: 2 * NE], spec[2 * NE :]
            gr, gi = g_spec[c, : 2 * NE], g_spec[c, 2 * NE :]
            both = jnp.concatenate([gr * sr - gi * si, gr * si + gi * sr], axis=0)
            upper = both.astype(BF16)
            lower = (both - upper.astype(F32)).astype(BF16)
            back = jnp.concatenate([table[k * B : (k + 1) * B] for k in (2, 3, 4)], axis=1)
            sums = dot(back, jnp.concatenate([upper, lower, upper], axis=0))
            for r in range(4):
                stage[pl.ds(r, NE, stride=8), :] = sums[:NE, r * B : (r + 1) * B]
                stage[pl.ds(r + 4, NE, stride=8), :] = sums[NE:, r * B : (r + 1) * B]
            c_send[c] = stage[...].reshape(NE, 8, B).astype(BF16)
        swap(c_send, c_recv, 4 + k, k, back=True)
    edges([g_next], [g_prev], "wait_recv")

    def place(packed, row, band):
        re, im = unpack(packed.astype(F32))
        s4[row, band, 0] = re.astype(BF16)
        s4[row, band, 1] = im.astype(BF16)

    for k in range(2):
        wait_swap(c_recv, 4 + k, k, back=True)
        edges(c_nexts[k : k + 1], c_prevs[k : k + 1], "start")
        for c in members[k]:
            place(c_recv[c, pl.ds(0, HALF)], 1, c)
            place(c_recv[c, pl.ds(HALF, HALF)], 2, 2 - c)
    for k in range(2):
        edges(c_nexts[k : k + 1], c_prevs[k : k + 1], "wait_recv")
        for c in members[k]:
            place(c_prev[c], 0, 2 - c)
            place(c_next[c], 3, c)
    for half in range(2):
        products = products_row(g4, s4, 1 + half)
        for band in range(3):
            block = close_row(products, g4, 1 + half, band)
            out_ref[half, band, 0] = block[:, :B].astype(BF16)
            out_ref[half, band, 1] = block[:, B:].astype(BF16)

    edges([w_next, p_next, g_next, *c_nexts], [w_prev, p_prev, g_prev, *c_prevs], "wait_send")
    wait_all_sent(g_send, 0)
    for k in range(2):
        wait_sent(s_send, 2 + k, k)
        wait_sent(c_send, 4 + k, k, back=True)


def local(screening, polarization, propagator):
    table = tables((3.0 * B / NE) ** 0.5)
    four = pltpu.VMEM((4, 3, 2, B, B), BF16)
    full = pltpu.VMEM((3, NE, 8, B), BF16)
    rim = pltpu.VMEM((3, HALF, 8, B), BF16)
    hbm = pl.BlockSpec(memory_space=pltpu.HBM)
    vmem = pl.BlockSpec(memory_space=pltpu.VMEM)
    out = pl.pallas_call(
        kernel,
        name="self_energy",
        out_shape=jax.ShapeDtypeStruct((2, 3, 2, B, B), BF16),
        in_specs=[hbm, hbm, hbm, hbm],
        out_specs=vmem,
        scratch_shapes=[
            four, four, four, four,
            full, full, full, full, full, full, rim, rim,
            pltpu.VMEM((5 * B, 2 * B), BF16),
            pltpu.VMEM((3, 4 * NE, 4 * B), F32),
            pltpu.VMEM((NE * 8, B), F32),
            pltpu.SemaphoreType.DMA((4,)),
            pltpu.SemaphoreType.DMA((10,)),
            pltpu.SemaphoreType.DMA((10,)),
            pltpu.SemaphoreType.DMA((6,)),
            pltpu.SemaphoreType.DMA((6,)),
        ],
        compiler_params=pltpu.CompilerParams(
            collective_id=0, has_side_effects=True, vmem_limit_bytes=54848 << 10
        ),
    )(screening[0], polarization[0], propagator[0], jnp.asarray(table))
    return out[None]


def solution(mesh):
    spec = P("energy", "space", None, None, None, None)
    return jax.shard_map(
        local, mesh=mesh, in_specs=(spec, spec, spec), out_specs=spec, check_vma=False
    )
```

```python
import math

import jax
import jax.numpy as jnp
import ml_dtypes
import numpy as np
from jax import lax
from jax.experimental import pallas as pl
from jax.experimental.pallas import tpu as pltpu
from jax.sharding import PartitionSpec as P

MESH = pl.DeviceIdType.MESH
B = 128
NE = 64
NS = 4
HALF = NE // 2
F32 = jnp.float32
BF16 = jnp.bfloat16


def split_np(table):
    upper = table.astype(ml_dtypes.bfloat16)
    lower = (table - upper.astype(np.float64)).astype(ml_dtypes.bfloat16)
    return upper, lower


def tables(factor):
    freq = np.arange(2 * NE)
    time = np.arange(NE)
    angle = (freq[:, None] * time[None, :] % (2 * NE)) * (math.pi / NE)
    cos, sin = np.cos(angle), np.sin(angle)
    fwd = np.block([[cos, sin], [-sin, cos]])
    back = np.block([[cos.T, -sin.T], [sin.T, cos.T]]) * (factor / (2 * NE))
    fh, fl = split_np(fwd)
    bh, bl = split_np(back)
    table = np.zeros((8 * B, 2 * B), ml_dtypes.bfloat16)
    table[: 5 * B] = np.concatenate([np.concatenate([fh, fl], 1), bh, bh, bl], 0)
    return table


def dot(a, b):
    return jnp.dot(a, b, preferred_element_type=F32)


def dot_nt(a, b):
    return lax.dot_general(a, b, (((1,), (1,)), ((), ())), preferred_element_type=F32)


def wide(ref, row, band):
    return jnp.concatenate([ref[row, band, 0], ref[row, band, 1]], axis=1)


def embed(ref, row, band):
    re, im = ref[row, band, 0], ref[row, band, 1]
    return jnp.concatenate(
        [jnp.concatenate([re, im], axis=1), jnp.concatenate([-im, re], axis=1)], axis=0
    )


def products_row(outer, inner, row):
    products = {}
    for offset in range(-2, 3):
        steps = [k for k in (-1, 0, 1) if abs(offset - k) <= 1]
        lhs = jnp.concatenate([wide(outer, row, k + 1) for k in steps], axis=1)
        rhs = jnp.concatenate([embed(inner, row + k, offset - k + 1) for k in steps], axis=0)
        products[offset] = dot(lhs, rhs).astype(BF16)
    return products


def close_row(products, outer, row, band):
    offsets = range(band - 2, band + 1)
    lhs = jnp.concatenate([products[d] for d in offsets], axis=1)
    rhs = jnp.concatenate([embed(outer, row + band - 1, d - band + 2) for d in offsets], axis=1)
    return dot_nt(lhs, rhs)


def pack(re, im):
    re, im = re.reshape(16, 8, B), im.reshape(16, 8, B)
    low = lax.broadcasted_iota(jnp.int32, (16, 8, B), 1) < 4
    even = jnp.where(low, re, pltpu.roll(im, 4, 1))
    odd = jnp.where(low, pltpu.roll(re, 4, 1), im)
    return jnp.stack([even, odd], axis=1).reshape(HALF, 8, B)


def unpack(packed):
    pairs = packed.reshape(16, 2, 8, B)
    even, odd = pairs[:, 0], pairs[:, 1]
    low = lax.broadcasted_iota(jnp.int32, (16, 8, B), 1) < 4
    re = jnp.where(low, even, pltpu.roll(odd, 4, 1))
    im = jnp.where(low, pltpu.roll(even, 4, 1), odd)
    return re.reshape(B, B), im.reshape(B, B)


def kernel(
    w_hbm, p_hbm, g_hbm, table_hbm, out_ref,
    w4, p4, g4, s4, g_send, g_recv, s_send, s_recv, c_send, c_recv, c_prev, c_next,
    table, g_spec, stage, load_sem, edge_send, edge_recv, swap_send, swap_recv,
):
    e = lax.axis_index("energy")
    s = lax.axis_index("space")
    barrier = pltpu.get_barrier_semaphore()
    loads = [
        pltpu.make_async_copy(src, dst.at[pl.ds(1, 2)], load_sem.at[i])
        for i, (src, dst) in enumerate(((g_hbm, g4), (w_hbm, w4), (p_hbm, p4)))
    ]
    table_loads = [
        pltpu.make_async_copy(table_hbm.at[pl.ds(0, 5 * B)], table, load_sem.at[3]),
    ]
    for load in loads + table_loads:
        load.start()

    def greet(i, carry):
        pl.semaphore_signal(barrier, inc=1, device_id=(lax.rem(e + i, NE), s), device_id_type=MESH)
        return carry

    @pl.when(s > 0)
    def _():
        pl.semaphore_signal(barrier, inc=1, device_id=(e, s - 1), device_id_type=MESH)

    @pl.when(s < NS - 1)
    def _():
        pl.semaphore_signal(barrier, inc=1, device_id=(e, s + 1), device_id_type=MESH)

    lax.fori_loop(1, NE, greet, 0)

    first, last = s == 0, s == NS - 1
    low = e < HALF
    idle = (first & low) | (last & jnp.logical_not(low))
    for load in loads:
        load.wait()

    @pl.when(first)
    def _():
        for ref in (w4, p4, g4):
            ref[0] = jnp.zeros(ref.shape[1:], BF16)
            ref[1, 0] = jnp.zeros(ref.shape[2:], BF16)
        c_prev[...] = jnp.zeros(c_prev.shape, BF16)
        c_recv[0, :HALF] = jnp.zeros((HALF, 8, B), BF16)

    @pl.when(last)
    def _():
        for ref in (w4, p4, g4):
            ref[3] = jnp.zeros(ref.shape[1:], BF16)
            ref[2, 2] = jnp.zeros(ref.shape[2:], BF16)
        c_next[...] = jnp.zeros(c_next.shape, BF16)
        c_recv[0, HALF:] = jnp.zeros((HALF, 8, B), BF16)

    pl.semaphore_wait(barrier, NE - 1 + (s > 0).astype(jnp.int32) + (s < NS - 1).astype(jnp.int32))

    def to_next(src, dst, i):
        return pltpu.make_async_remote_copy(
            src, dst, edge_send.at[i], edge_recv.at[i], device_id=(e, s + 1), device_id_type=MESH
        )

    def to_prev(src, dst, i):
        return pltpu.make_async_remote_copy(
            src, dst, edge_send.at[i], edge_recv.at[i], device_id=(e, s - 1), device_id_type=MESH
        )

    groups = (pl.ds(1, 2), pl.ds(0, 1))
    w_next, w_prev = to_next(w4.at[2], w4.at[0], 0), to_prev(w4.at[1], w4.at[3], 1)
    p_next, p_prev = to_next(p4.at[2], p4.at[0], 2), to_prev(p4.at[1], p4.at[3], 3)
    g_next, g_prev = to_next(g4.at[2], g4.at[0], 4), to_prev(g4.at[1], g4.at[3], 5)
    c_nexts = [
        to_next(c_recv.at[part, pl.ds(HALF, HALF)], c_prev.at[part], 6 + k)
        for k, part in enumerate(groups)
    ]
    c_prevs = [
        to_prev(c_recv.at[part, pl.ds(0, HALF)], c_next.at[part], 8 + k)
        for k, part in enumerate(groups)
    ]

    def edges(nexts, prevs, action):
        forward, backward = (prevs, nexts) if action == "wait_recv" else (nexts, prevs)

        @pl.when(s < NS - 1)
        def _():
            for copy in forward:
                getattr(copy, action)()

        @pl.when(s > 0)
        def _():
            for copy in backward:
                getattr(copy, action)()

    def swap(send, recv, slot, k, back=False):
        part = groups[k]

        def body(i, carry):
            to = lax.rem(e + i, NE)
            copy = pltpu.make_async_remote_copy(
                send.at[part, to], recv.at[part, e], swap_send.at[slot], swap_recv.at[slot],
                device_id=(to, s), device_id_type=MESH,
            )
            if k == 0 or back:
                copy.start()
            else:
                nothing = (first & (to < HALF)) | (last & (to >= HALF))

                @pl.when(jnp.logical_not(nothing))
                def _():
                    copy.start()

            return carry

        def run():
            lax.fori_loop(1, NE, body, 0)
            own = pltpu.make_async_copy(send.at[part, e], recv.at[part, e], swap_recv.at[slot])
            own.start()

        if k == 0:
            run()
        elif back:
            pl.when(jnp.logical_not(idle))(run)
        else:
            lax.fori_loop(1, NE, body, 0)

            @pl.when(jnp.logical_not(idle))
            def _():
                pltpu.make_async_copy(
                    send.at[part, e], recv.at[part, e], swap_recv.at[slot]
                ).start()

    def swap_all(send, recv, slot):
        def copy(part, to):
            return pltpu.make_async_remote_copy(
                send.at[part, to], recv.at[part, e], swap_send.at[slot], swap_recv.at[slot],
                device_id=(to, s), device_id_type=MESH,
            )

        def body(i, carry):
            to = lax.rem(e + i, NE)
            nothing = (first & (to < HALF)) | (last & (to >= HALF))

            @pl.when(nothing)
            def _():
                copy(pl.ds(1, 2), to).start()

            @pl.when(jnp.logical_not(nothing))
            def _():
                copy(pl.ds(0, 3), to).start()

            return carry

        lax.fori_loop(1, NE, body, 0)

        @pl.when(idle)
        def _():
            own = pl.ds(1, 2)
            pltpu.make_async_copy(send.at[own, e], recv.at[own, e], swap_recv.at[slot]).start()

        @pl.when(jnp.logical_not(idle))
        def _():
            pltpu.make_async_copy(send.at[:, e], recv.at[:, e], swap_recv.at[slot]).start()

    def wait_all(recv, slot):
        sem = swap_recv.at[slot]

        @pl.when(idle)
        def _():
            pltpu.make_async_copy(recv.at[pl.ds(1, 2)], recv.at[pl.ds(1, 2)], sem).wait()

        @pl.when(jnp.logical_not(idle))
        def _():
            pltpu.make_async_copy(recv, recv, sem).wait()

    def wait_all_sent(send, slot):
        sem = swap_send.at[slot]
        pair = send.at[pl.ds(1, 2), pl.ds(0, NE - 1)]
        pltpu.make_async_copy(pair, pair, sem).wait()
        ends = first | last
        pl.when(jnp.logical_not(ends))(lambda: finish(send, sem, NE - 1, 1))
        pl.when(idle)(lambda: finish(send, sem, HALF, 1))
        pl.when(ends & jnp.logical_not(idle))(lambda: finish(send, sem, HALF - 1, 1))

    def finish(ref, sem, count, k):
        full = ref.at[groups[k], pl.ds(0, count)]
        pltpu.make_async_copy(full, full, sem).wait()

    def wait_swap(recv, slot, k, back=False):
        sem = swap_recv.at[slot]
        if k == 0:
            finish(recv, sem, NE, k)
        elif back:
            ends = first | last
            pl.when(ends)(lambda: finish(recv, sem, HALF, k))
            pl.when(jnp.logical_not(ends))(lambda: finish(recv, sem, NE, k))
        else:
            pl.when(jnp.logical_not(idle))(lambda: finish(recv, sem, NE, k))

    def wait_sent(send, slot, k, back=False):
        sem = swap_send.at[slot]
        if k == 0:
            finish(send, sem, NE - 1, k)
        elif back:
            pl.when(jnp.logical_not(idle))(lambda: finish(send, sem, NE - 1, k))
        else:
            ends = first | last
            pl.when(jnp.logical_not(ends))(lambda: finish(send, sem, NE - 1, k))
            pl.when(idle)(lambda: finish(send, sem, HALF, k))
            pl.when(ends & jnp.logical_not(idle))(lambda: finish(send, sem, HALF - 1, k))

    members = ((1, 2), (0,))
    edges([w_next, p_next], [w_prev, p_prev], "start")
    for c in range(3):
        for half in range(2):
            band = c if half == 0 else 2 - c
            re = g4[1 + half, band, 0].astype(F32)
            im = g4[1 + half, band, 1].astype(F32)
            g_send[c, pl.ds(half * HALF, HALF)] = pack(re, im).astype(BF16)
    @pl.when(jnp.logical_not(first | last))
    def _():
        swap_all(g_send, g_recv, 0)


    @pl.when(idle)
    def _():
        g_recv[0] = jnp.zeros(g_recv.shape[1:], BF16)
        s_recv[0] = jnp.zeros(s_recv.shape[1:], BF16)

    edges([w_next, p_next], [w_prev, p_prev], "wait_recv")
    firsts = [products_row(w4, p4, 1 + half) for half in range(2)]
    for k in range(2):
        for c in members[k]:
            for half in range(2):
                band = c if half == 0 else 2 - c
                block = close_row(firsts[half], w4, 1 + half, band)
                s_send[c, pl.ds(half * HALF, HALF)] = pack(block[:, :B], block[:, B:]).astype(BF16)
        swap(s_send, s_recv, 2 + k, k)
    @pl.when(first | last)
    def _():
        swap_all(g_send, g_recv, 0)

    edges([g_next], [g_prev], "start")

    def spectrum(recv, c):
        stage[...] = recv[c].astype(F32).reshape(NE * 8, B)
        rows = [stage[pl.ds(r, NE, stride=8), :].astype(BF16) for r in range(8)]
        data = jnp.concatenate(
            [jnp.concatenate(rows[:4], axis=1), jnp.concatenate(rows[4:], axis=1)], axis=0
        )
        return dot(table[: 2 * B], jnp.concatenate([data, data], axis=0))

    for load in table_loads:
        load.wait()
    wait_all(g_recv, 0)
    for c in range(3):
        g_spec[c] = spectrum(g_recv, c)
    for k in range(2):
        wait_swap(s_recv, 2 + k, k)
        for c in members[k]:
            spec = spectrum(s_recv, c)
            sr, si = spec[: 2 * NE], spec[2 * NE :]
            gr, gi = g_spec[c, : 2 * NE], g_spec[c, 2 * NE :]
            both = jnp.concatenate([gr * sr - gi * si, gr * si + gi * sr], axis=0)
            upper = both.astype(BF16)
            lower = (both - upper.astype(F32)).astype(BF16)
            back = jnp.concatenate([table[k * B : (k + 1) * B] for k in (2, 3, 4)], axis=1)
            sums = dot(back, jnp.concatenate([upper, lower, upper], axis=0))
            for r in range(4):
                stage[pl.ds(r, NE, stride=8), :] = sums[:NE, r * B : (r + 1) * B]
                stage[pl.ds(r + 4, NE, stride=8), :] = sums[NE:, r * B : (r + 1) * B]
            c_send[c] = stage[...].reshape(NE, 8, B).astype(BF16)
        swap(c_send, c_recv, 4 + k, k, back=True)
    edges([g_next], [g_prev], "wait_recv")

    def place(packed, row, band):
        re, im = unpack(packed.astype(F32))
        s4[row, band, 0] = re.astype(BF16)
        s4[row, band, 1] = im.astype(BF16)

    for k in range(2):
        wait_swap(c_recv, 4 + k, k, back=True)
        edges(c_nexts[k : k + 1], c_prevs[k : k + 1], "start")
        for c in members[k]:
            place(c_recv[c, pl.ds(0, HALF)], 1, c)
            place(c_recv[c, pl.ds(HALF, HALF)], 2, 2 - c)
    def take_prev():
        @pl.when(s > 0)
        def _():
            for copy in c_nexts:
                copy.wait_recv()

        for c in range(3):
            place(c_prev[c], 0, 2 - c)

    def take_next():
        @pl.when(s < NS - 1)
        def _():
            for copy in c_prevs:
                copy.wait_recv()

        for c in range(3):
            place(c_next[c], 3, c)

    def dress(half):
        products = products_row(g4, s4, 1 + half)
        for band in range(3):
            block = close_row(products, g4, 1 + half, band)
            out_ref[half, band, 0] = block[:, :B].astype(BF16)
            out_ref[half, band, 1] = block[:, B:].astype(BF16)

    near = (s >= NS // 2).astype(jnp.int32)
    pl.when(near == 0)(take_prev)
    pl.when(near == 1)(take_next)
    dress(near)
    pl.when(near == 0)(take_next)
    pl.when(near == 1)(take_prev)
    dress(1 - near)

    edges([w_next, p_next, g_next, *c_nexts], [w_prev, p_prev, g_prev, *c_prevs], "wait_send")
    wait_all_sent(g_send, 0)
    for k in range(2):
        wait_sent(s_send, 2 + k, k)
        wait_sent(c_send, 4 + k, k, back=True)


def local(screening, polarization, propagator):
    table = tables((3.0 * B / NE) ** 0.5)
    four = pltpu.VMEM((4, 3, 2, B, B), BF16)
    full = pltpu.VMEM((3, NE, 8, B), BF16)
    rim = pltpu.VMEM((3, HALF, 8, B), BF16)
    hbm = pl.BlockSpec(memory_space=pltpu.HBM)
    vmem = pl.BlockSpec(memory_space=pltpu.VMEM)
    out = pl.pallas_call(
        kernel,
        name="self_energy",
        out_shape=jax.ShapeDtypeStruct((2, 3, 2, B, B), BF16),
        in_specs=[hbm, hbm, hbm, hbm],
        out_specs=vmem,
        scratch_shapes=[
            four, four, four, four,
            full, full, full, full, full, full, rim, rim,
            pltpu.VMEM((5 * B, 2 * B), BF16),
            pltpu.VMEM((3, 4 * NE, 4 * B), F32),
            pltpu.VMEM((NE * 8, B), F32),
            pltpu.SemaphoreType.DMA((4,)),
            pltpu.SemaphoreType.DMA((10,)),
            pltpu.SemaphoreType.DMA((10,)),
            pltpu.SemaphoreType.DMA((6,)),
            pltpu.SemaphoreType.DMA((6,)),
        ],
        compiler_params=pltpu.CompilerParams(
            collective_id=0, has_side_effects=True, vmem_limit_bytes=54848 << 10
        ),
    )(screening[0], polarization[0], propagator[0], jnp.asarray(table))
    return out[None]


def solution(mesh):
    spec = P("energy", "space", None, None, None, None)
    return jax.shard_map(
        local, mesh=mesh, in_specs=(spec, spec, spec), out_specs=spec, check_vma=False
    )
```

```python
import math

import jax
import jax.numpy as jnp
import ml_dtypes
import numpy as np
from jax import lax
from jax.experimental import pallas as pl
from jax.experimental.pallas import tpu as pltpu
from jax.sharding import PartitionSpec as P

MESH = pl.DeviceIdType.MESH
B = 128
NE = 64
NS = 4
HALF = NE // 2
F32 = jnp.float32
BF16 = jnp.bfloat16


def split_np(table):
    upper = table.astype(ml_dtypes.bfloat16)
    lower = (table - upper.astype(np.float64)).astype(ml_dtypes.bfloat16)
    return upper, lower


def tables(factor):
    freq = np.arange(2 * NE)
    time = np.arange(NE)
    angle = (freq[:, None] * time[None, :] % (2 * NE)) * (math.pi / NE)
    cos, sin = np.cos(angle), np.sin(angle)
    fwd = np.block([[cos, sin], [-sin, cos]])
    back = np.block([[cos.T, -sin.T], [sin.T, cos.T]]) * (factor / (2 * NE))
    fh, fl = split_np(fwd)
    bh, bl = split_np(back)
    table = np.zeros((8 * B, 2 * B), ml_dtypes.bfloat16)
    table[: 5 * B] = np.concatenate([np.concatenate([fh, fl], 1), bh, bh, bl], 0)
    return table


def dot(a, b):
    return jnp.dot(a, b, preferred_element_type=F32)


def dot_nt(a, b):
    return lax.dot_general(a, b, (((1,), (1,)), ((), ())), preferred_element_type=F32)


def wide(ref, row, band):
    return jnp.concatenate([ref[row, band, 0], ref[row, band, 1]], axis=1)


def embed(ref, row, band):
    re, im = ref[row, band, 0], ref[row, band, 1]
    return jnp.concatenate(
        [jnp.concatenate([re, im], axis=1), jnp.concatenate([-im, re], axis=1)], axis=0
    )


def products_row(outer, inner, row):
    products = {}
    for offset in range(-2, 3):
        steps = [k for k in (-1, 0, 1) if abs(offset - k) <= 1]
        lhs = jnp.concatenate([wide(outer, row, k + 1) for k in steps], axis=1)
        rhs = jnp.concatenate([embed(inner, row + k, offset - k + 1) for k in steps], axis=0)
        products[offset] = dot(lhs, rhs).astype(BF16)
    return products


def close_row(products, outer, row, band):
    offsets = range(band - 2, band + 1)
    lhs = jnp.concatenate([products[d] for d in offsets], axis=1)
    rhs = jnp.concatenate([embed(outer, row + band - 1, d - band + 2) for d in offsets], axis=1)
    return dot_nt(lhs, rhs)


def pack(re, im):
    re, im = re.reshape(16, 8, B), im.reshape(16, 8, B)
    low = lax.broadcasted_iota(jnp.int32, (16, 8, B), 1) < 4
    even = jnp.where(low, re, pltpu.roll(im, 4, 1))
    odd = jnp.where(low, pltpu.roll(re, 4, 1), im)
    return jnp.stack([even, odd], axis=1).reshape(HALF, 8, B)


def unpack(packed):
    pairs = packed.reshape(16, 2, 8, B)
    even, odd = pairs[:, 0], pairs[:, 1]
    low = lax.broadcasted_iota(jnp.int32, (16, 8, B), 1) < 4
    re = jnp.where(low, even, pltpu.roll(odd, 4, 1))
    im = jnp.where(low, pltpu.roll(even, 4, 1), odd)
    return re.reshape(B, B), im.reshape(B, B)


def kernel(
    w_hbm, p_hbm, g_hbm, table_hbm, out_ref,
    w4, p4, g4, s4, g_send, g_recv, s_send, s_recv, c_send, c_recv, c_prev, c_next,
    table, g_spec, stage, load_sem, edge_send, edge_recv, swap_send, swap_recv,
):
    e = lax.axis_index("energy")
    s = lax.axis_index("space")
    barrier = pltpu.get_barrier_semaphore()
    loads = [
        pltpu.make_async_copy(src, dst.at[pl.ds(1, 2)], load_sem.at[i])
        for i, (src, dst) in enumerate(((g_hbm, g4), (w_hbm, w4), (p_hbm, p4)))
    ]
    table_loads = [
        pltpu.make_async_copy(table_hbm.at[pl.ds(0, 5 * B)], table, load_sem.at[3]),
    ]
    def greet(i, carry):
        pl.semaphore_signal(barrier, inc=1, device_id=(lax.rem(e + i, NE), s), device_id_type=MESH)
        return carry

    @pl.when(s > 0)
    def _():
        pl.semaphore_signal(barrier, inc=1, device_id=(e, s - 1), device_id_type=MESH)

    @pl.when(s < NS - 1)
    def _():
        pl.semaphore_signal(barrier, inc=1, device_id=(e, s + 1), device_id_type=MESH)

    lax.fori_loop(1, NE, greet, 0)
    for load in loads + table_loads:
        load.start()

    first, last = s == 0, s == NS - 1
    low = e < HALF
    idle = (first & low) | (last & jnp.logical_not(low))
    pl.semaphore_wait(barrier, NE - 1 + (s > 0).astype(jnp.int32) + (s < NS - 1).astype(jnp.int32))

    def to_next(src, dst, i):
        return pltpu.make_async_remote_copy(
            src, dst, edge_send.at[i], edge_recv.at[i], device_id=(e, s + 1), device_id_type=MESH
        )

    def to_prev(src, dst, i):
        return pltpu.make_async_remote_copy(
            src, dst, edge_send.at[i], edge_recv.at[i], device_id=(e, s - 1), device_id_type=MESH
        )

    groups = (pl.ds(1, 2), pl.ds(0, 1))
    w_next, w_prev = to_next(w_hbm.at[1], w4.at[0], 0), to_prev(w_hbm.at[0], w4.at[3], 1)
    p_next, p_prev = to_next(p_hbm.at[1], p4.at[0], 2), to_prev(p_hbm.at[0], p4.at[3], 3)
    g_next, g_prev = to_next(g4.at[2], g4.at[0], 4), to_prev(g4.at[1], g4.at[3], 5)
    c_nexts = [
        to_next(c_recv.at[part, pl.ds(HALF, HALF)], c_prev.at[part], 6 + k)
        for k, part in enumerate(groups)
    ]
    c_prevs = [
        to_prev(c_recv.at[part, pl.ds(0, HALF)], c_next.at[part], 8 + k)
        for k, part in enumerate(groups)
    ]

    def edges(nexts, prevs, action):
        forward, backward = (prevs, nexts) if action == "wait_recv" else (nexts, prevs)

        @pl.when(s < NS - 1)
        def _():
            for copy in forward:
                getattr(copy, action)()

        @pl.when(s > 0)
        def _():
            for copy in backward:
                getattr(copy, action)()

    def swap(send, recv, slot, k, back=False):
        part = groups[k]

        def body(i, carry):
            to = lax.rem(e + i, NE)
            copy = pltpu.make_async_remote_copy(
                send.at[part, to], recv.at[part, e], swap_send.at[slot], swap_recv.at[slot],
                device_id=(to, s), device_id_type=MESH,
            )
            if k == 0 or back:
                copy.start()
            else:
                nothing = (first & (to < HALF)) | (last & (to >= HALF))

                @pl.when(jnp.logical_not(nothing))
                def _():
                    copy.start()

            return carry

        def run():
            lax.fori_loop(1, NE, body, 0)
            own = pltpu.make_async_copy(send.at[part, e], recv.at[part, e], swap_recv.at[slot])
            own.start()

        if k == 0:
            run()
        elif back:
            pl.when(jnp.logical_not(idle))(run)
        else:
            lax.fori_loop(1, NE, body, 0)

            @pl.when(jnp.logical_not(idle))
            def _():
                pltpu.make_async_copy(
                    send.at[part, e], recv.at[part, e], swap_recv.at[slot]
                ).start()

    def swap_all(send, recv, slot):
        def copy(part, to):
            return pltpu.make_async_remote_copy(
                send.at[part, to], recv.at[part, e], swap_send.at[slot], swap_recv.at[slot],
                device_id=(to, s), device_id_type=MESH,
            )

        def body(i, carry):
            to = lax.rem(e + i, NE)
            nothing = (first & (to < HALF)) | (last & (to >= HALF))

            @pl.when(nothing)
            def _():
                copy(pl.ds(1, 2), to).start()

            @pl.when(jnp.logical_not(nothing))
            def _():
                copy(pl.ds(0, 3), to).start()

            return carry

        lax.fori_loop(1, NE, body, 0)

        @pl.when(idle)
        def _():
            own = pl.ds(1, 2)
            pltpu.make_async_copy(send.at[own, e], recv.at[own, e], swap_recv.at[slot]).start()

        @pl.when(jnp.logical_not(idle))
        def _():
            pltpu.make_async_copy(send.at[:, e], recv.at[:, e], swap_recv.at[slot]).start()

    def wait_all(recv, slot):
        sem = swap_recv.at[slot]

        @pl.when(idle)
        def _():
            pltpu.make_async_copy(recv.at[pl.ds(1, 2)], recv.at[pl.ds(1, 2)], sem).wait()

        @pl.when(jnp.logical_not(idle))
        def _():
            pltpu.make_async_copy(recv, recv, sem).wait()

    def wait_all_sent(send, slot):
        sem = swap_send.at[slot]
        pair = send.at[pl.ds(1, 2), pl.ds(0, NE - 1)]
        pltpu.make_async_copy(pair, pair, sem).wait()
        ends = first | last
        pl.when(jnp.logical_not(ends))(lambda: finish(send, sem, NE - 1, 1))
        pl.when(idle)(lambda: finish(send, sem, HALF, 1))
        pl.when(ends & jnp.logical_not(idle))(lambda: finish(send, sem, HALF - 1, 1))

    def finish(ref, sem, count, k):
        full = ref.at[groups[k], pl.ds(0, count)]
        pltpu.make_async_copy(full, full, sem).wait()

    def wait_swap(recv, slot, k, back=False):
        sem = swap_recv.at[slot]
        if k == 0:
            finish(recv, sem, NE, k)
        elif back:
            ends = first | last
            pl.when(ends)(lambda: finish(recv, sem, HALF, k))
            pl.when(jnp.logical_not(ends))(lambda: finish(recv, sem, NE, k))
        else:
            pl.when(jnp.logical_not(idle))(lambda: finish(recv, sem, NE, k))

    def wait_sent(send, slot, k, back=False):
        sem = swap_send.at[slot]
        if k == 0:
            finish(send, sem, NE - 1, k)
        elif back:
            pl.when(jnp.logical_not(idle))(lambda: finish(send, sem, NE - 1, k))
        else:
            ends = first | last
            pl.when(jnp.logical_not(ends))(lambda: finish(send, sem, NE - 1, k))
            pl.when(idle)(lambda: finish(send, sem, HALF, k))
            pl.when(ends & jnp.logical_not(idle))(lambda: finish(send, sem, HALF - 1, k))

    members = ((1, 2), (0,))
    edges([w_next, p_next], [w_prev, p_prev], "start")
    for load in loads:
        load.wait()

    @pl.when(first)
    def _():
        for ref in (w4, p4, g4):
            ref[0] = jnp.zeros(ref.shape[1:], BF16)
            ref[1, 0] = jnp.zeros(ref.shape[2:], BF16)
        c_prev[...] = jnp.zeros(c_prev.shape, BF16)
        c_recv[0, :HALF] = jnp.zeros((HALF, 8, B), BF16)

    @pl.when(last)
    def _():
        for ref in (w4, p4, g4):
            ref[3] = jnp.zeros(ref.shape[1:], BF16)
            ref[2, 2] = jnp.zeros(ref.shape[2:], BF16)
        c_next[...] = jnp.zeros(c_next.shape, BF16)
        c_recv[0, HALF:] = jnp.zeros((HALF, 8, B), BF16)

    for c in range(3):
        for half in range(2):
            band = c if half == 0 else 2 - c
            re = g4[1 + half, band, 0].astype(F32)
            im = g4[1 + half, band, 1].astype(F32)
            g_send[c, pl.ds(half * HALF, HALF)] = pack(re, im).astype(BF16)
    @pl.when(jnp.logical_not(first | last))
    def _():
        swap_all(g_send, g_recv, 0)


    @pl.when(idle)
    def _():
        g_recv[0] = jnp.zeros(g_recv.shape[1:], BF16)
        s_recv[0] = jnp.zeros(s_recv.shape[1:], BF16)

    edges([w_next, p_next], [w_prev, p_prev], "wait_recv")
    firsts = [products_row(w4, p4, 1 + half) for half in range(2)]
    for k in range(2):
        for c in members[k]:
            for half in range(2):
                band = c if half == 0 else 2 - c
                block = close_row(firsts[half], w4, 1 + half, band)
                s_send[c, pl.ds(half * HALF, HALF)] = pack(block[:, :B], block[:, B:]).astype(BF16)
        swap(s_send, s_recv, 2 + k, k)
    @pl.when(first | last)
    def _():
        swap_all(g_send, g_recv, 0)

    edges([g_next], [g_prev], "start")

    def spectrum(recv, c):
        stage[...] = recv[c].astype(F32).reshape(NE * 8, B)
        rows = [stage[pl.ds(r, NE, stride=8), :].astype(BF16) for r in range(8)]
        data = jnp.concatenate(
            [jnp.concatenate(rows[:4], axis=1), jnp.concatenate(rows[4:], axis=1)], axis=0
        )
        return dot(table[: 2 * B], jnp.concatenate([data, data], axis=0))

    for load in table_loads:
        load.wait()
    wait_all(g_recv, 0)
    for c in range(3):
        g_spec[c] = spectrum(g_recv, c)
    for k in range(2):
        wait_swap(s_recv, 2 + k, k)
        for c in members[k]:
            spec = spectrum(s_recv, c)
            sr, si = spec[: 2 * NE], spec[2 * NE :]
            gr, gi = g_spec[c, : 2 * NE], g_spec[c, 2 * NE :]
            both = jnp.concatenate([gr * sr - gi * si, gr * si + gi * sr], axis=0)
            upper = both.astype(BF16)
            lower = (both - upper.astype(F32)).astype(BF16)
            back = jnp.concatenate([table[k * B : (k + 1) * B] for k in (2, 3, 4)], axis=1)
            sums = dot(back, jnp.concatenate([upper, lower, upper], axis=0))
            for r in range(4):
                stage[pl.ds(r, NE, stride=8), :] = sums[:NE, r * B : (r + 1) * B]
                stage[pl.ds(r + 4, NE, stride=8), :] = sums[NE:, r * B : (r + 1) * B]
            c_send[c] = stage[...].reshape(NE, 8, B).astype(BF16)
        swap(c_send, c_recv, 4 + k, k, back=True)
    edges([g_next], [g_prev], "wait_recv")

    def place(packed, row, band):
        re, im = unpack(packed.astype(F32))
        s4[row, band, 0] = re.astype(BF16)
        s4[row, band, 1] = im.astype(BF16)

    for k in range(2):
        wait_swap(c_recv, 4 + k, k, back=True)
        edges(c_nexts[k : k + 1], c_prevs[k : k + 1], "start")
        for c in members[k]:
            place(c_recv[c, pl.ds(0, HALF)], 1, c)
            place(c_recv[c, pl.ds(HALF, HALF)], 2, 2 - c)
    def take_prev():
        @pl.when(s > 0)
        def _():
            for copy in c_nexts:
                copy.wait_recv()

        for c in range(3):
            place(c_prev[c], 0, 2 - c)

    def take_next():
        @pl.when(s < NS - 1)
        def _():
            for copy in c_prevs:
                copy.wait_recv()

        for c in range(3):
            place(c_next[c], 3, c)

    def dress(half):
        products = products_row(g4, s4, 1 + half)
        for band in range(3):
            block = close_row(products, g4, 1 + half, band)
            out_ref[half, band, 0] = block[:, :B].astype(BF16)
            out_ref[half, band, 1] = block[:, B:].astype(BF16)

    near = (s >= NS // 2).astype(jnp.int32)
    pl.when(near == 0)(take_prev)
    pl.when(near == 1)(take_next)
    dress(near)
    pl.when(near == 0)(take_next)
    pl.when(near == 1)(take_prev)
    dress(1 - near)

    edges([w_next, p_next, g_next, *c_nexts], [w_prev, p_prev, g_prev, *c_prevs], "wait_send")
    wait_all_sent(g_send, 0)
    for k in range(2):
        wait_sent(s_send, 2 + k, k)
        wait_sent(c_send, 4 + k, k, back=True)


def local(screening, polarization, propagator):
    table = tables((3.0 * B / NE) ** 0.5)
    four = pltpu.VMEM((4, 3, 2, B, B), BF16)
    full = pltpu.VMEM((3, NE, 8, B), BF16)
    rim = pltpu.VMEM((3, HALF, 8, B), BF16)
    hbm = pl.BlockSpec(memory_space=pltpu.HBM)
    vmem = pl.BlockSpec(memory_space=pltpu.VMEM)
    out = pl.pallas_call(
        kernel,
        name="self_energy",
        out_shape=jax.ShapeDtypeStruct((2, 3, 2, B, B), BF16),
        in_specs=[hbm, hbm, hbm, hbm],
        out_specs=vmem,
        scratch_shapes=[
            four, four, four, four,
            full, full, full, full, full, full, rim, rim,
            pltpu.VMEM((5 * B, 2 * B), BF16),
            pltpu.VMEM((3, 4 * NE, 4 * B), F32),
            pltpu.VMEM((NE * 8, B), F32),
            pltpu.SemaphoreType.DMA((4,)),
            pltpu.SemaphoreType.DMA((10,)),
            pltpu.SemaphoreType.DMA((10,)),
            pltpu.SemaphoreType.DMA((6,)),
            pltpu.SemaphoreType.DMA((6,)),
        ],
        compiler_params=pltpu.CompilerParams(
            collective_id=0, has_side_effects=True, vmem_limit_bytes=54848 << 10
        ),
    )(screening[0], polarization[0], propagator[0], jnp.asarray(table))
    return out[None]


def solution(mesh):
    spec = P("energy", "space", None, None, None, None)
    return jax.shard_map(
        local, mesh=mesh, in_specs=(spec, spec, spec), out_specs=spec, check_vma=False
    )
```
